32 devices in a mesh: dom: 16 (over z, y, x), feat: 2 (over core).
Axes of the slice: x: 2, y: 2, z: 4, core: 2. Of those that a mesh axis runs over, the one named last changes fastest.
Arguments:
- features: bfloat16 [2048, 128], P('dom'), may hold values from -6 to 6
- w_self: bfloat16 [128, 256], P(None, 'feat'), may hold values from -0.5 to 0.5
- w_neigh: bfloat16 [128, 256], P(None, 'feat'), may hold values from -6 to 6
- tiles: bfloat16 [256, 128, 128], P('dom'), may hold values from 0 to 1, as said below
- dest: int32 [256, 1], P('dom'), may hold values from 0 to 15; in each aligned block of 16 rows (0 to 15, 16 to 31, ...) at most 2 rows name the same one
- outside: int32 [2048], P('dom'), may hold values from 1 to 256
- cotangent: bfloat16 [2048, 256], P('dom', 'feat'), may hold values from -6 to 6
Outputs:
- output: bfloat16 [2048, 256], P('dom', 'feat')
- grad_input: bfloat16 [2048, 128], P('dom')
- grad_self: float32 [128, 256], P(None, 'feat')
- grad_neigh: float32 [128, 256], P(None, 'feat')
The draws below stay inside these ranges and needn't reach their ends.
Inputs may be any that keep to these rules, and one draw needn't show every extreme that they name: `dest`: among the 16 tiles of one index of dom, at most 2 name one destination block, and some block is named by exactly 2. `tiles`: entries are 0 or 1.
All inputs are finite; a program needn't handle non-finite values.
Results may differ from the reference program's by a relative error of at most 0.015.
Values may be sent and summed in bfloat16 or wider, within the bound.
No kernel may reach another device: no remote copies, remote signals or barrier semaphores. Data moves between devices by JAX's collectives and lax.ppermute only.
A program may use at most 128 MiB of HBM per device.

```python
import math
import jax
import jax.numpy as jnp
import numpy as np
from jax import lax

FIN = 128
HID = 256
BLOCK = 128
CAP = 2
TILES_DEV = 16
NODES = 2048
TILES = 256
N_DOM = 16


def draw_tiles(key, part):
    key = jax.random.fold_in(key, 11)
    links = jax.random.bernoulli(key, 2.0 / BLOCK, (TILES, BLOCK, BLOCK))
    return links.astype(jnp.float32).astype(jnp.bfloat16)


def set_ends(values, own_key, least, largest):
    spot = [jax.random.randint(jax.random.fold_in(own_key, axis), (), 0, length) for axis, length in enumerate(values.shape)]
    widest = values.shape.index(max(values.shape))
    neighbour = spot[:widest] + [(spot[widest] + 1) % values.shape[widest]] + spot[widest + 1:]
    return values.at[tuple(spot)].set(least).at[tuple(neighbour)].set(largest)


def levels(rng, shape, split, smallest, top_value):
    level = 1.0
    for position, parts in split:
        heights = jax.random.uniform(jax.random.fold_in(jax.random.fold_in(rng, 6), position), (parts,), jnp.float32, smallest / len(split), top_value / len(split))
        level = level * jnp.repeat(jnp.exp(heights), shape[position] // parts).reshape((-1,) + (1,) * (len(shape) - 1 - position))
    return level


def shared_out(own_key, own, number, rows, count, top, most, skew):
    order = jax.random.permutation(own_key, count)
    crowded, usual = portions_of(count, rows * top, most, skew, True), portions_of(count, rows * top, most, skew, False)
    places = jnp.arange(count)

    def named(tallies, offset_by):
        used = int((tallies > 0).sum())
        fixed = max(1, used // 4)
        moved = fixed + (places - fixed + offset_by * (used - fixed)) % max(1, count - fixed)
        return jnp.zeros((count,), jnp.int32).at[order[jnp.where(places < fixed, places, moved)]].set(jnp.asarray(tallies, jnp.int32))

    tallies = jnp.where(number % 4 == 0, named(crowded, number // 4), named(usual, number - number // 4 - 1))
    mixed = jax.random.permutation(jax.random.fold_in(own, 3), count)
    source_of, sink = mixed[0:count // 2 * 2:2], mixed[1:count // 2 * 2:2]
    margin = jnp.minimum(tallies[source_of] - 1, most - tallies[sink]) // 2
    margin = jnp.where((source_of == order[0]) | (sink == order[0]) | (tallies[sink] == 0), 0, jnp.maximum(margin, 0))
    moved = jax.random.randint(jax.random.fold_in(own, 4), (count // 2,), 0, 1 << 20) % (margin + 1)
    tallies = tallies.at[source_of].add(-moved).at[sink].add(moved)
    items = jnp.searchsorted(jnp.cumsum(tallies), jnp.arange(rows * top), side="right").astype(jnp.int32)
    table = items.reshape(top, rows).T
    table = table[jax.random.permutation(jax.random.fold_in(own, 1), rows)]
    offset_by = jax.random.randint(jax.random.fold_in(own, 2), (rows, 1), 0, top)
    return jnp.take_along_axis(table, (jnp.arange(top)[None, :] + offset_by) % top, axis=1)


def portions_of(amount, total, bound, lean, full):
    portions = [(1 << 20) // math.isqrt(standing ** lean) + 1 for standing in range(1, amount + 1)]
    largest = bound if full else min(bound, max(-(-total // amount), total * portions[0] // sum(portions)))
    least = 1 if total - largest >= amount - 1 else 0
    given, surplus = [largest] + [least] * (amount - 1), total - largest - least * (amount - 1)
    while surplus > 0:
        candidates = [i for i in range(1, amount) if given[i] < largest] or [i for i in range(1, amount) if given[i] < bound]
        mass, budget = sum([portions[i] for i in candidates]), surplus
        for i in candidates:
            more = min(bound - given[i], max(1, budget * portions[i] // mass), surplus)
            given[i] = given[i] + more
            surplus = surplus - more
    return np.array(given)


def noise(stream_key, extent, width, limit, pieces=(), held_as=jnp.bfloat16):
    result = width * jax.random.normal(stream_key, extent, jnp.float32)
    if pieces:
        result = result * levels(stream_key, extent, pieces, -0.22, 0.18)
    return jnp.clip(result, -limit, limit).astype(held_as)


def setup_inputs(seed: int = 0) -> dict:
    splits = jax.random.split(jax.random.key(seed), 8)
    features = noise(splits[0], (NODES, FIN), 1.0, 6.0, ((0, 16),))
    w_self = noise(splits[1], (FIN, HID), FIN ** -0.5, 0.5, ((1, 2),))
    w_neigh = noise(splits[2], (FIN, HID), 1.0, 6.0, ((1, 2),))
    tiles = draw_tiles(jax.random.fold_in(splits[7], 71), 0)
    dest_keys = jax.random.split(jax.random.fold_in(splits[4], 1), TILES // TILES_DEV)
    dest_turns = jax.random.permutation(jax.random.fold_in(splits[4], 3), TILES // TILES_DEV)
    dest = jax.vmap(lambda own, number: shared_out(jax.random.fold_in(splits[4], 2), own, number, TILES_DEV, N_DOM, 1, CAP, 2))(dest_keys, dest_turns).reshape((TILES, 1))
    outside = set_ends(jax.random.randint(splits[5], (NODES,), 1, 257), jax.random.fold_in(splits[5], 1), 1, 256).astype(jnp.int32)
    cotangent = noise(splits[6], (NODES, HID), 1.0, 6.0, ((0, 16), (1, 2)))
    return {"features": features, "w_self": w_self, "w_neigh": w_neigh, "tiles": tiles, "dest": dest, "outside": outside, "cotangent": cotangent}


def reference(features, w_self, w_neigh, tiles, dest, outside, cotangent):
    self_part = jnp.dot(features, w_self, preferred_element_type=jnp.float32)
    message = jnp.dot(features, w_neigh, preferred_element_type=jnp.float32).astype(jnp.bfloat16)
    msg_blocks = message.reshape(N_DOM, BLOCK, HID)
    tile_groups = tiles.reshape(N_DOM, TILES_DEV, BLOCK, BLOCK)
    dest_groups = dest.reshape(N_DOM, TILES_DEV).astype(jnp.int32)

    def forward_step(carry, inputs):
        total, link_total = carry
        group, targets, block_rows = inputs
        group_f = group.astype(jnp.float32)
        partial_sum = jnp.einsum("tij,ik->tjk", group_f, block_rows.astype(jnp.float32))
        column_sums = jnp.sum(group_f, axis=1)
        return (total.at[targets].add(partial_sum), link_total.at[targets].add(column_sums)), None

    start = (jnp.zeros((N_DOM, BLOCK, HID), jnp.float32), jnp.zeros((N_DOM, BLOCK), jnp.float32))
    (summed, links), _ = lax.scan(forward_step, start, (tile_groups, dest_groups, msg_blocks))
    inverse = 1.0 / (links.reshape(NODES) + outside.astype(jnp.float32))
    pre = self_part + summed.reshape(NODES, HID) * inverse[:, None]
    sigma = jax.nn.sigmoid(pre)
    output = (pre * sigma).astype(jnp.bfloat16)
    dpre = (cotangent.astype(jnp.float32) * sigma * (1.0 + pre * (1.0 - sigma))).astype(jnp.bfloat16)
    dagg = (dpre.astype(jnp.float32) * inverse[:, None]).astype(jnp.bfloat16)
    dagg_blocks = dagg.reshape(N_DOM, BLOCK, HID)

    def backward_step(carry, inputs):
        group, targets = inputs
        fetched = dagg_blocks[targets]
        return carry, jnp.einsum("tij,tjk->ik", group.astype(jnp.float32), fetched.astype(jnp.float32))

    _, dmessage = lax.scan(backward_step, jnp.float32(0.0), (tile_groups, dest_groups))
    dmessage = dmessage.reshape(NODES, HID).astype(jnp.bfloat16)
    grad_self = jnp.dot(features.T, dpre, preferred_element_type=jnp.float32)
    grad_neigh = jnp.dot(features.T, dmessage, preferred_element_type=jnp.float32)
    grad_input = (jnp.dot(dpre, w_self.T, preferred_element_type=jnp.float32) + jnp.dot(dmessage, w_neigh.T, preferred_element_type=jnp.float32)).astype(jnp.bfloat16)
    return output, grad_input, grad_self, grad_neigh
```

```python
import jax
import jax.numpy as jnp
from jax import lax
from jax.experimental import pallas as pl
from jax.experimental.pallas import tpu as pltpu
from jax.sharding import PartitionSpec as P

BF16 = jnp.bfloat16
F32 = jnp.float32
EXTRA = 8
MIB = 1 << 20

NN = (((1,), (0,)), ((), ()))
NT = (((1,), (1,)), ((), ()))


def dot(a, b, dims):
    return lax.dot_general(a, b, dims, preferred_element_type=F32)


def loop(count, body):
    if count <= 16:
        for index in range(count):
            body(index)
    else:
        pl.loop(0, count)(body)


def listed(index, peers):
    bits = peers.bit_length() - 1
    index = index ^ (peers - 1)
    return sum(((index >> bit) & 1) << (bits - 1 - bit) for bit in range(bits))


def halves(size):
    core = lax.axis_index("feat")
    half = size // 2
    return pl.ds(pl.multiple_of(core * half, half), half), pl.ds(pl.multiple_of((1 - core) * half, half), half)


def share_kernel(
    dest_hbm, features_hbm, tiles_hbm, share_ref, dest_ref, features_ref, tiles_ref, turned_ref, sums_ref, sems,
):
    copies = [
        pltpu.make_async_copy(source, target, sems.at[i])
        for i, (source, target) in enumerate(
            [(features_hbm, features_ref), (dest_hbm, dest_ref), (tiles_hbm, tiles_ref)]
        )
    ]
    for copy in copies:
        copy.start()
    peers = sums_ref.shape[0]
    sums_ref[...] = jnp.zeros_like(sums_ref)
    copies[0].wait()
    turned_ref[...] = features_ref[...].T
    own, _ = halves(turned_ref.shape[0])
    left = jnp.concatenate([turned_ref[own, :], jnp.ones((EXTRA, turned_ref.shape[1]), BF16)], axis=0)
    copies[1].wait()
    copies[2].wait()

    def add(t):
        sums_ref[listed(dest_ref[t], peers)] += dot(left, tiles_ref[t], NN)

    loop(tiles_ref.shape[0], add)
    share_ref[...] = sums_ref[...].astype(BF16)


def sum_kernel(arrived_ref, w_self_ref, w_neigh_ref, cotangent_ref, total_ref, links_ref):
    half = arrived_ref.shape[1] - EXTRA
    fin = w_self_ref.shape[0]
    total = jnp.sum(arrived_ref[...].astype(F32), axis=0)
    links_ref[...] = total[half:]
    total_ref[:half] = total[:half].astype(BF16)
    total_ref[half : half + fin] = w_self_ref[...]
    total_ref[half + fin : half + 2 * fin] = w_neigh_ref[...]
    _, sibling = halves(cotangent_ref.shape[0])
    total_ref[half + 2 * fin :] = cotangent_ref[sibling, :]


def node_kernel(
    total_ref, other_ref, links_ref, outside_ref, features_ref, w_self_ref, w_neigh_ref, cotangent_ref,
    output_ref, packed_ref, term_ref, gathered_ref, nodes_ref, scale_ref, dagg_ref,
):
    fin, rows = gathered_ref.shape
    hidden = w_self_ref.shape[1]
    quarter = fin // 2
    own, sibling = halves(fin)
    low, _ = halves(rows)
    gathered_ref[own, :] = total_ref[:quarter]
    gathered_ref[sibling, :] = other_ref[:quarter]
    gathered = gathered_ref[...]
    nodes_ref[...] = gathered.T
    degree = links_ref[0:1] + outside_ref[...].astype(F32)
    scale_ref[...] = jnp.broadcast_to(1.0 / degree, (hidden, rows)).T

    def gradients(features, nodes, scale, w_self, w_neigh, cotangent):
        pre = dot(features, w_self, NN) + dot(nodes, w_neigh, NN) * scale
        sigma = 1.0 / (1.0 + jnp.exp(-pre))
        dpre = (cotangent.astype(F32) * sigma * (1.0 + pre * (1.0 - sigma))).astype(BF16)
        return pre * sigma, dpre, (dpre.astype(F32) * scale).astype(BF16)

    features, w_neigh = features_ref[...], w_neigh_ref[...]
    silu, dpre, dagg = gradients(
        features, nodes_ref[...], scale_ref[...], w_self_ref[...], w_neigh, cotangent_ref[...]
    )
    output_ref[...] = silu.astype(BF16)
    dagg_ref[...] = dagg
    w_self_other = other_ref[quarter : quarter + fin]
    w_neigh_other = other_ref[quarter + fin : quarter + 2 * fin]
    _, _, dagg_other = gradients(
        features_ref[low, :], nodes_ref[low, :], scale_ref[low, :], w_self_other, w_neigh_other,
        other_ref[quarter + 2 * fin :],
    )
    back = dot(dagg_ref[low, :], w_neigh, NT) + dot(dagg_other, w_neigh_other, NT)
    peers, packed, _ = packed_ref.shape
    slab = 2 * fin // peers
    half = rows // 2
    packed_ref[:, :half] = jnp.broadcast_to(back.astype(BF16)[None], (peers, half, fin))
    weight = jnp.concatenate([dot(features.T, dpre, NN), dot(gathered, dagg, NN)], axis=0)
    weight = weight.reshape(peers, slab, hidden)
    if packed - half > slab:
        weight = jnp.concatenate([weight, jnp.zeros((peers, packed - half - slab, hidden), F32)], axis=1)
    packed_ref[:, half:] = weight.astype(BF16)
    term_ref[...] = dot(dpre, w_self_ref[...], NT)


def input_kernel(dest_ref, back_ref, tiles_ref, term_ref, total_ref, padded_ref):
    own, sibling = halves(tiles_ref.shape[2])
    half = tiles_ref.shape[2] // 2
    peers = padded_ref.shape[0]
    padded_ref[:, own, :] = back_ref[:, :half]
    padded_ref[:, sibling, :] = jnp.zeros((padded_ref.shape[0], half, padded_ref.shape[2]), BF16)
    total = term_ref[...]
    if tiles_ref.shape[0] <= 16:
        for t in range(tiles_ref.shape[0]):
            total = total + dot(tiles_ref[t], padded_ref[listed(dest_ref[t], peers)], NN)
    else:
        total = lax.fori_loop(
            0, tiles_ref.shape[0], lambda t, sum: sum + dot(tiles_ref[t], padded_ref[listed(dest_ref[t], peers)], NN), total
        )
    total_ref[...] = total


def spread_kernel(part_ref, parts_ref):
    parts_ref[...] = jnp.broadcast_to(part_ref[...][None], parts_ref.shape)


def output_kernel(silu_ref, term_ref, other_ref, weight_ref, output_ref, grad_input_ref, grad_self_ref, grad_neigh_ref):
    output_ref[...] = silu_ref[...]
    fin = grad_self_ref.shape[0]
    grad_input_ref[...] = (term_ref[...] + other_ref[...]).astype(BF16)
    grad_self_ref[...] = weight_ref[:fin].astype(F32)
    grad_neigh_ref[...] = weight_ref[fin:].astype(F32)


def on_device(features, w_self, w_neigh, tiles, dest, outside, cotangent):
    peers = lax.axis_size("dom")
    tile_count, rows, _ = tiles.shape
    fin, hidden = w_self.shape
    half = fin // 2
    slab = 2 * fin // peers
    smem = pl.BlockSpec(memory_space=pltpu.SMEM)
    vmem = pl.BlockSpec(memory_space=pltpu.VMEM)
    hbm = pl.BlockSpec(memory_space=pltpu.HBM)
    targets = dest.reshape(-1)
    shape = jax.ShapeDtypeStruct

    def swap(x):
        return lax.ppermute(x, "feat", [(0, 1), (1, 0)])

    group = sorted(range(peers), key=lambda index: listed(index, peers))

    def exchange(x):
        return lax.all_to_all(x, "dom", split_axis=0, concat_axis=0, tiled=True, axis_index_groups=[group])

    extended = half + EXTRA
    share = pl.pallas_call(
        share_kernel,
        out_shape=pltpu.VMEM((peers, extended, rows), BF16),
        in_specs=[hbm] * 3,
        out_specs=vmem,
        scratch_shapes=[
            pltpu.SMEM((tile_count,), jnp.int32),
            pltpu.VMEM((rows, fin), BF16),
            pltpu.VMEM(tiles.shape, BF16),
            pltpu.VMEM((fin, rows), BF16),
            pltpu.VMEM((peers, extended, rows), F32),
            pltpu.SemaphoreType.DMA((3,)),
        ],
        compiler_params=pltpu.CompilerParams(vmem_limit_bytes=60 * MIB),
        name="share",
    )(targets, features, tiles)
    arrived = exchange(share)
    together = half + 2 * fin + rows // 2
    total, links = pl.pallas_call(
        sum_kernel,
        out_shape=(pltpu.VMEM((together, hidden), BF16), pltpu.VMEM((EXTRA, rows), F32)),
        in_specs=[vmem] * 4,
        out_specs=(vmem,) * 2,
        compiler_params=pltpu.CompilerParams(vmem_limit_bytes=(4 + peers // 8) * MIB),
        name="sum",
    )(arrived, w_self, w_neigh, cotangent)
    output, packed, term = pl.pallas_call(
        node_kernel,
        out_shape=(
            pltpu.VMEM((rows, hidden), BF16),
            pltpu.VMEM((peers, rows // 2 + max(slab, 16), hidden), BF16),
            shape((rows, fin), F32),
        ),
        in_specs=[vmem] * 8,
        out_specs=(vmem,) * 3,
        scratch_shapes=[
            pltpu.VMEM((fin, rows), BF16),
            pltpu.VMEM((rows, fin), BF16),
            pltpu.VMEM((rows, hidden), F32),
            pltpu.VMEM((rows, hidden), BF16),
        ],
        compiler_params=pltpu.CompilerParams(vmem_limit_bytes=(4 + peers // 8) * MIB),
        name="node",
    )(total, swap(total), links, outside.reshape(1, rows), features, w_self, w_neigh, cotangent)
    back = exchange(packed)
    summed = jnp.sum(back[:, rows // 2 : rows // 2 + slab].astype(F32), axis=0).astype(BF16)
    summed = pl.pallas_call(
        spread_kernel,
        out_shape=pltpu.VMEM((peers, slab, hidden), BF16),
        in_specs=[vmem],
        out_specs=vmem,
        compiler_params=pltpu.CompilerParams(vmem_limit_bytes=4 * MIB),
        name="spread",
    )(summed)
    summed, back = lax.optimization_barrier((summed, back))
    weight = exchange(summed)
    term = pl.pallas_call(
        input_kernel,
        out_shape=shape((rows, fin), F32),
        in_specs=[smem] + [vmem] * 3,
        out_specs=vmem,
        scratch_shapes=[pltpu.VMEM((peers, rows, fin), BF16)],
        compiler_params=pltpu.CompilerParams(vmem_limit_bytes=(4 + peers // 8) * MIB),
        name="input",
    )(targets, back, tiles, term)
    block = shape((fin, hidden), F32)
    return pl.pallas_call(
        output_kernel,
        out_shape=(shape((rows, hidden), BF16), shape((rows, fin), BF16), block, block),
        in_specs=[vmem] * 4,
        out_specs=(vmem,) * 4,
        compiler_params=pltpu.CompilerParams(vmem_limit_bytes=4 * MIB),
        name="outputs",
    )(output, term, swap(term), weight.reshape(2 * fin, hidden))


def solution(mesh):
    placed = (
        P("dom", None),
        P(None, "feat"),
        P(None, "feat"),
        P("dom", None, None),
        P("dom", None),
        P("dom"),
        P("dom", "feat"),
    )
    return jax.shard_map(
        on_device,
        mesh=mesh,
        in_specs=placed,
        out_specs=(P("dom", "feat"), P("dom", None), P(None, "feat"), P(None, "feat")),
        check_vma=False,
    )
```

```python
import jax
import jax.numpy as jnp
from jax import lax
from jax.experimental import pallas as pl
from jax.experimental.pallas import tpu as pltpu
from jax.sharding import PartitionSpec as P

BF16 = jnp.bfloat16
F32 = jnp.float32
EXTRA = 8
MIB = 1 << 20

NN = (((1,), (0,)), ((), ()))
NT = (((1,), (1,)), ((), ()))


def dot(a, b, dims):
    return lax.dot_general(a, b, dims, preferred_element_type=F32)


def loop(count, body):
    if count <= 16:
        for index in range(count):
            body(index)
    else:
        pl.loop(0, count)(body)


def listed(index, peers):
    bits = peers.bit_length() - 1
    index = index ^ (peers - peers // 4 - 1)
    return sum(((index >> bit) & 1) << (bits - 1 - bit) for bit in range(bits))


def halves(size):
    core = lax.axis_index("feat")
    half = size // 2
    return pl.ds(pl.multiple_of(core * half, half), half), pl.ds(pl.multiple_of((1 - core) * half, half), half)


def share_kernel(
    dest_hbm, features_hbm, outside_hbm, tiles_hbm, share_ref, outside_ref, dest_ref, features_ref, tiles_ref, turned_ref, sums_ref, sems,
):
    copies = [
        pltpu.make_async_copy(source, target, sems.at[i])
        for i, (source, target) in enumerate(
            [(features_hbm, features_ref), (dest_hbm, dest_ref), (tiles_hbm, tiles_ref), (outside_hbm, outside_ref)]
        )
    ]
    for copy in copies:
        copy.start()
    peers = sums_ref.shape[0]
    sums_ref[...] = jnp.zeros_like(sums_ref)
    copies[0].wait()
    turned_ref[...] = features_ref[...].T
    own, _ = halves(turned_ref.shape[0])
    left = jnp.concatenate([turned_ref[own, :], jnp.ones((EXTRA, turned_ref.shape[1]), BF16)], axis=0)
    copies[1].wait()
    copies[2].wait()

    def add(t):
        sums_ref[listed(dest_ref[t], peers)] += dot(left, tiles_ref[t], NN)

    loop(tiles_ref.shape[0], add)
    share_ref[...] = sums_ref[...].astype(BF16)
    copies[3].wait()


def sum_kernel(arrived_ref, w_self_ref, w_neigh_ref, cotangent_ref, total_ref, links_ref):
    half = arrived_ref.shape[1] - EXTRA
    fin = w_self_ref.shape[0]
    total = jnp.sum(arrived_ref[...].astype(F32), axis=0)
    links_ref[...] = total[half:]
    total_ref[:half] = total[:half].astype(BF16)
    total_ref[half : half + fin] = w_self_ref[...]
    total_ref[half + fin : half + 2 * fin] = w_neigh_ref[...]
    _, sibling = halves(cotangent_ref.shape[0])
    total_ref[half + 2 * fin :] = cotangent_ref[sibling, :]


def node_kernel(
    total_ref, other_ref, links_ref, outside_ref, features_ref, w_self_ref, w_neigh_ref, cotangent_ref,
    output_ref, packed_ref, term_ref, gathered_ref, nodes_ref, scale_ref, dagg_ref,
):
    fin, rows = gathered_ref.shape
    hidden = w_self_ref.shape[1]
    quarter = fin // 2
    own, sibling = halves(fin)
    low, _ = halves(rows)
    gathered_ref[own, :] = total_ref[:quarter]
    gathered_ref[sibling, :] = other_ref[:quarter]
    gathered = gathered_ref[...]
    nodes_ref[...] = gathered.T
    degree = links_ref[0:1] + outside_ref[...].astype(F32)
    scale_ref[...] = jnp.broadcast_to(1.0 / degree, (hidden, rows)).T

    def gradients(features, nodes, scale, w_self, w_neigh, cotangent):
        pre = dot(features, w_self, NN) + dot(nodes, w_neigh, NN) * scale
        sigma = 1.0 / (1.0 + jnp.exp(-pre))
        dpre = (cotangent.astype(F32) * sigma * (1.0 + pre * (1.0 - sigma))).astype(BF16)
        return pre * sigma, dpre, (dpre.astype(F32) * scale).astype(BF16)

    features, w_neigh = features_ref[...], w_neigh_ref[...]
    silu, dpre, dagg = gradients(
        features, nodes_ref[...], scale_ref[...], w_self_ref[...], w_neigh, cotangent_ref[...]
    )
    output_ref[...] = silu.astype(BF16)
    dagg_ref[...] = dagg
    w_self_other = other_ref[quarter : quarter + fin]
    w_neigh_other = other_ref[quarter + fin : quarter + 2 * fin]
    _, _, dagg_other = gradients(
        features_ref[low, :], nodes_ref[low, :], scale_ref[low, :], w_self_other, w_neigh_other,
        other_ref[quarter + 2 * fin :],
    )
    back = dot(dagg_ref[low, :], w_neigh, NT) + dot(dagg_other, w_neigh_other, NT)
    peers, packed, _ = packed_ref.shape
    slab = 2 * fin // peers
    half = rows // 2
    packed_ref[:, :half] = jnp.broadcast_to(back.astype(BF16)[None], (peers, half, fin))
    weight = jnp.concatenate([dot(features.T, dpre, NN), dot(gathered, dagg, NN)], axis=0)
    weight = weight.reshape(peers, slab, hidden)
    if packed - half > slab:
        weight = jnp.concatenate([weight, jnp.zeros((peers, packed - half - slab, hidden), F32)], axis=1)
    packed_ref[:, half:] = weight.astype(BF16)
    term_ref[...] = dot(dpre, w_self_ref[...], NT)


def input_kernel(dest_ref, back_ref, tiles_ref, term_ref, total_ref, padded_ref):
    own, sibling = halves(tiles_ref.shape[2])
    half = tiles_ref.shape[2] // 2
    peers = padded_ref.shape[0]
    padded_ref[:, own, :] = back_ref[:, :half]
    padded_ref[:, sibling, :] = jnp.zeros((padded_ref.shape[0], half, padded_ref.shape[2]), BF16)
    total = term_ref[...]
    if tiles_ref.shape[0] <= 16:
        for t in range(tiles_ref.shape[0]):
            total = total + dot(tiles_ref[t], padded_ref[listed(dest_ref[t], peers)], NN)
    else:
        total = lax.fori_loop(
            0, tiles_ref.shape[0], lambda t, sum: sum + dot(tiles_ref[t], padded_ref[listed(dest_ref[t], peers)], NN), total
        )
    total_ref[...] = total


def spread_kernel(part_ref, parts_ref):
    parts_ref[...] = jnp.broadcast_to(part_ref[...][None], parts_ref.shape)


def output_kernel(silu_ref, term_ref, other_ref, weight_ref, output_ref, grad_input_ref, grad_self_ref, grad_neigh_ref):
    output_ref[...] = silu_ref[...]
    fin = grad_self_ref.shape[0]
    grad_input_ref[...] = (term_ref[...] + other_ref[...]).astype(BF16)
    grad_self_ref[...] = weight_ref[:fin].astype(F32)
    grad_neigh_ref[...] = weight_ref[fin:].astype(F32)


def on_device(features, w_self, w_neigh, tiles, dest, outside, cotangent):
    peers = lax.axis_size("dom")
    tile_count, rows, _ = tiles.shape
    fin, hidden = w_self.shape
    half = fin // 2
    slab = 2 * fin // peers
    smem = pl.BlockSpec(memory_space=pltpu.SMEM)
    vmem = pl.BlockSpec(memory_space=pltpu.VMEM)
    hbm = pl.BlockSpec(memory_space=pltpu.HBM)
    targets = dest.reshape(-1)
    shape = jax.ShapeDtypeStruct

    def swap(x):
        return lax.ppermute(x, "feat", [(0, 1), (1, 0)])

    group = sorted(range(peers), key=lambda index: listed(index, peers))

    def exchange(x):
        return lax.all_to_all(x, "dom", split_axis=0, concat_axis=0, tiled=True, axis_index_groups=[group])

    extended = half + EXTRA
    share, outside = pl.pallas_call(
        share_kernel,
        out_shape=(pltpu.VMEM((peers, extended, rows), BF16), pltpu.VMEM((1, rows), jnp.int32)),
        in_specs=[hbm] * 4,
        out_specs=(vmem, vmem),
        scratch_shapes=[
            pltpu.SMEM((tile_count,), jnp.int32),
            pltpu.VMEM((rows, fin), BF16),
            pltpu.VMEM(tiles.shape, BF16),
            pltpu.VMEM((fin, rows), BF16),
            pltpu.VMEM((peers, extended, rows), F32),
            pltpu.SemaphoreType.DMA((4,)),
        ],
        compiler_params=pltpu.CompilerParams(vmem_limit_bytes=60 * MIB),
        name="share",
    )(targets, features, outside.reshape(1, rows), tiles)
    arrived = exchange(share)
    together = half + 2 * fin + rows // 2
    total, links = pl.pallas_call(
        sum_kernel,
        out_shape=(pltpu.VMEM((together, hidden), BF16), pltpu.VMEM((EXTRA, rows), F32)),
        in_specs=[vmem] * 4,
        out_specs=(vmem,) * 2,
        compiler_params=pltpu.CompilerParams(vmem_limit_bytes=(4 + peers // 8) * MIB),
        name="sum",
    )(arrived, w_self, w_neigh, cotangent)
    output, packed, term = pl.pallas_call(
        node_kernel,
        out_shape=(
            pltpu.VMEM((rows, hidden), BF16),
            pltpu.VMEM((peers, rows // 2 + max(slab, 16), hidden), BF16),
            shape((rows, fin), F32),
        ),
        in_specs=[vmem] * 8,
        out_specs=(vmem,) * 3,
        scratch_shapes=[
            pltpu.VMEM((fin, rows), BF16),
            pltpu.VMEM((rows, fin), BF16),
            pltpu.VMEM((rows, hidden), F32),
            pltpu.VMEM((rows, hidden), BF16),
        ],
        compiler_params=pltpu.CompilerParams(vmem_limit_bytes=(4 + peers // 8) * MIB),
        name="node",
    )(total, swap(total), links, outside, features, w_self, w_neigh, cotangent)
    back = exchange(packed)
    summed = jnp.sum(back[:, rows // 2 : rows // 2 + slab].astype(F32), axis=0).astype(BF16)
    summed = pl.pallas_call(
        spread_kernel,
        out_shape=pltpu.VMEM((peers, slab, hidden), BF16),
        in_specs=[vmem],
        out_specs=vmem,
        compiler_params=pltpu.CompilerParams(vmem_limit_bytes=4 * MIB),
        name="spread",
    )(summed)
    summed, back = lax.optimization_barrier((summed, back))
    weight = exchange(summed)
    term = pl.pallas_call(
        input_kernel,
        out_shape=shape((rows, fin), F32),
        in_specs=[smem] + [vmem] * 3,
        out_specs=vmem,
        scratch_shapes=[pltpu.VMEM((peers, rows, fin), BF16)],
        compiler_params=pltpu.CompilerParams(vmem_limit_bytes=(4 + peers // 8) * MIB),
        name="input",
    )(targets, back, tiles, term)
    block = shape((fin, hidden), F32)
    return pl.pallas_call(
        output_kernel,
        out_shape=(shape((rows, hidden), BF16), shape((rows, fin), BF16), block, block),
        in_specs=[vmem] * 4,
        out_specs=(vmem,) * 4,
        compiler_params=pltpu.CompilerParams(vmem_limit_bytes=4 * MIB),
        name="outputs",
    )(output, term, swap(term), weight.reshape(2 * fin, hidden))


def solution(mesh):
    placed = (
        P("dom", None),
        P(None, "feat"),
        P(None, "feat"),
        P("dom", None, None),
        P("dom", None),
        P("dom"),
        P("dom", "feat"),
    )
    return jax.shard_map(
        on_device,
        mesh=mesh,
        in_specs=placed,
        out_specs=(P("dom", "feat"), P("dom", None), P(None, "feat"), P(None, "feat")),
        check_vma=False,
    )
```

```python
import jax
import jax.numpy as jnp
from jax import lax
from jax.experimental import pallas as pl
from jax.experimental.pallas import tpu as pltpu
from jax.sharding import PartitionSpec as P

BF16 = jnp.bfloat16
F32 = jnp.float32
EXTRA = 8
SHARERS = 2
MIB = 1 << 20

NN = (((1,), (0,)), ((), ()))
NT = (((1,), (1,)), ((), ()))


def dot(a, b, dims):
    return lax.dot_general(a, b, dims, preferred_element_type=F32)


def loop(count, body):
    if count <= 16:
        for index in range(count):
            body(index)
    else:
        pl.loop(0, count)(body)


def listed(index, peers, corner=False):
    bits = peers.bit_length() - 1
    index = index ^ (peers - 1 if corner else peers - peers // 4 - 1)
    return sum(((index >> bit) & 1) << (bits - 1 - bit) for bit in range(bits))


def halves(size):
    core = lax.axis_index("feat")
    half = size // 2
    return pl.ds(pl.multiple_of(core * half, half), half), pl.ds(pl.multiple_of((1 - core) * half, half), half)


def share_kernel(
    dest_hbm, features_hbm, outside_hbm, tiles_hbm, share_ref, outside_ref, targets_ref, dest_ref, features_ref, tiles_ref, turned_ref, sums_ref, sems,
):
    copies = [
        pltpu.make_async_copy(source, target, sems.at[i])
        for i, (source, target) in enumerate(
            [(features_hbm, features_ref), (dest_hbm, dest_ref), (tiles_hbm, tiles_ref), (outside_hbm, outside_ref), (dest_hbm, targets_ref)]
        )
    ]
    for copy in copies:
        copy.start()
    peers = sums_ref.shape[0]
    sums_ref[...] = jnp.zeros_like(sums_ref)
    copies[0].wait()
    turned_ref[...] = features_ref[...].T
    own, _ = halves(turned_ref.shape[0])
    left = jnp.concatenate([turned_ref[own, :], jnp.ones((EXTRA, turned_ref.shape[1]), BF16)], axis=0)
    copies[1].wait()
    copies[2].wait()

    def add(t):
        sums_ref[listed(dest_ref[t], peers)] += dot(left, tiles_ref[t], NN)

    loop(tiles_ref.shape[0], add)
    share_ref[...] = sums_ref[...].astype(BF16)
    copies[3].wait()
    copies[4].wait()


def sum_kernel(arrived_ref, w_self_ref, w_neigh_ref, cotangent_ref, total_ref, links_ref):
    half = arrived_ref.shape[1] - EXTRA
    fin = w_self_ref.shape[0]
    total = jnp.sum(arrived_ref[...].astype(F32), axis=0)
    links_ref[...] = total[half:]
    total_ref[:half] = total[:half].astype(BF16)
    total_ref[half : half + fin] = w_self_ref[...]
    total_ref[half + fin : half + 2 * fin] = w_neigh_ref[...]
    _, sibling = halves(cotangent_ref.shape[0])
    total_ref[half + 2 * fin :] = cotangent_ref[sibling, :]


def node_kernel(
    total_ref, other_ref, links_ref, outside_ref, features_ref, w_self_ref, w_neigh_ref, cotangent_ref,
    output_ref, packed_ref, term_ref, gathered_ref, nodes_ref, scale_ref, dagg_ref,
):
    fin, rows = gathered_ref.shape
    hidden = w_self_ref.shape[1]
    quarter = fin // 2
    own, sibling = halves(fin)
    low, _ = halves(rows)
    gathered_ref[own, :] = total_ref[:quarter]
    gathered_ref[sibling, :] = other_ref[:quarter]
    gathered = gathered_ref[...]
    nodes_ref[...] = gathered.T
    degree = links_ref[0:1] + outside_ref[...].astype(F32)
    scale_ref[...] = jnp.broadcast_to(1.0 / degree, (hidden, rows)).T

    def gradients(features, nodes, scale, w_self, w_neigh, cotangent):
        pre = dot(features, w_self, NN) + dot(nodes, w_neigh, NN) * scale
        sigma = 1.0 / (1.0 + jnp.exp(-pre))
        dpre = (cotangent.astype(F32) * sigma * (1.0 + pre * (1.0 - sigma))).astype(BF16)
        return pre * sigma, dpre, (dpre.astype(F32) * scale).astype(BF16)

    features, w_neigh = features_ref[...], w_neigh_ref[...]
    silu, dpre, dagg = gradients(
        features, nodes_ref[...], scale_ref[...], w_self_ref[...], w_neigh, cotangent_ref[...]
    )
    output_ref[...] = silu.astype(BF16)
    dagg_ref[...] = dagg
    w_self_other = other_ref[quarter : quarter + fin]
    w_neigh_other = other_ref[quarter + fin : quarter + 2 * fin]
    _, _, dagg_other = gradients(
        features_ref[low, :], nodes_ref[low, :], scale_ref[low, :], w_self_other, w_neigh_other,
        other_ref[quarter + 2 * fin :],
    )
    back = dot(dagg_ref[low, :], w_neigh, NT) + dot(dagg_other, w_neigh_other, NT)
    peers, packed, _ = packed_ref.shape
    owners = peers // SHARERS
    slab = 2 * fin // owners
    half = rows // 4
    back = back.astype(BF16)
    weight = jnp.concatenate([dot(features.T, dpre, NN), dot(gathered, dagg, NN)], axis=0)
    weight = weight.reshape(owners, slab, hidden)
    if packed - half > slab:
        weight = jnp.concatenate([weight, jnp.zeros((owners, packed - half - slab, hidden), F32)], axis=1)
    order = sorted(range(peers), key=lambda index: listed(index, peers))
    for k, index in enumerate(order):
        packed_ref[k, :half] = back[(index & 1) * half : (index & 1) * half + half]
        packed_ref[k, half:] = weight[listed(index % owners, owners, corner=True)].astype(BF16)
    term_ref[...] = dot(dpre, w_self_ref[...], NT)


def input_kernel(targets_ref, back_ref, pair_ref, tiles_ref, term_ref, total_ref, dest_ref, padded_ref, sem):
    copy = pltpu.make_async_copy(targets_ref, dest_ref, sem)
    copy.start()
    half = tiles_ref.shape[2] // 2
    _, sibling = halves(tiles_ref.shape[2])
    quarter = half // 2
    first = lax.axis_index("feat") * half
    odd = lax.axis_index("dom") & 1
    padded_ref[:, pl.ds(pl.multiple_of(first + odd * quarter, quarter), quarter), :] = back_ref[...]
    padded_ref[:, pl.ds(pl.multiple_of(first + (1 - odd) * quarter, quarter), quarter), :] = pair_ref[...]
    padded_ref[:, sibling, :] = jnp.zeros((padded_ref.shape[0], half, padded_ref.shape[2]), BF16)
    peers = padded_ref.shape[0]
    total = term_ref[...]
    copy.wait()
    if tiles_ref.shape[0] <= 16:
        for t in range(tiles_ref.shape[0]):
            total = total + dot(tiles_ref[t], padded_ref[listed(dest_ref[t], peers)], NN)
    else:
        total = lax.fori_loop(
            0, tiles_ref.shape[0], lambda t, sum: sum + dot(tiles_ref[t], padded_ref[listed(dest_ref[t], peers)], NN), total
        )
    total_ref[...] = total


def spread_kernel(back_ref, parts_ref):
    _, slab, _ = parts_ref.shape
    half = back_ref.shape[2] // 4
    part = jnp.sum(back_ref[:, half : half + slab].astype(F32), axis=0).astype(BF16)
    parts_ref[...] = jnp.broadcast_to(part[None], parts_ref.shape)


def output_kernel(silu_ref, term_ref, other_ref, weight_ref, output_ref, grad_input_ref, grad_self_ref, grad_neigh_ref):
    output_ref[...] = silu_ref[...]
    fin = grad_self_ref.shape[0]
    grad_input_ref[...] = (term_ref[...] + other_ref[...]).astype(BF16)
    grad_self_ref[...] = weight_ref[:fin].astype(F32)
    grad_neigh_ref[...] = weight_ref[fin:].astype(F32)


def on_device(features, w_self, w_neigh, tiles, dest, outside, cotangent):
    peers = lax.axis_size("dom")
    tile_count, rows, _ = tiles.shape
    fin, hidden = w_self.shape
    half = fin // 2
    slab = 2 * fin // (peers // SHARERS)
    vmem = pl.BlockSpec(memory_space=pltpu.VMEM)
    hbm = pl.BlockSpec(memory_space=pltpu.HBM)
    targets = dest.reshape(-1)
    shape = jax.ShapeDtypeStruct

    def swap(x):
        return lax.ppermute(x, "feat", [(0, 1), (1, 0)])

    def exchange(x, groups):
        return lax.all_to_all(x, "dom", split_axis=0, concat_axis=0, tiled=True, axis_index_groups=groups)

    middle = [sorted(range(peers), key=lambda index: listed(index, peers))]
    owners = peers // SHARERS
    corner = sorted(range(owners), key=lambda index: listed(index, owners, corner=True))
    corner = [[first + index for index in corner] for first in range(0, peers, owners)]
    extended = half + EXTRA
    share, outside, targets = pl.pallas_call(
        share_kernel,
        out_shape=(
            pltpu.VMEM((peers, extended, rows), BF16),
            pltpu.VMEM((1, rows), jnp.int32),
            pltpu.VMEM((tile_count,), jnp.int32),
        ),
        in_specs=[hbm] * 4,
        out_specs=(vmem,) * 3,
        scratch_shapes=[
            pltpu.SMEM((tile_count,), jnp.int32),
            pltpu.VMEM((rows, fin), BF16),
            pltpu.VMEM(tiles.shape, BF16),
            pltpu.VMEM((fin, rows), BF16),
            pltpu.VMEM((peers, extended, rows), F32),
            pltpu.SemaphoreType.DMA((5,)),
        ],
        compiler_params=pltpu.CompilerParams(vmem_limit_bytes=60 * MIB),
        name="share",
    )(targets, features, outside.reshape(1, rows), tiles)
    arrived = exchange(share, middle)
    together = half + 2 * fin + rows // 2
    total, links = pl.pallas_call(
        sum_kernel,
        out_shape=(pltpu.VMEM((together, hidden), BF16), pltpu.VMEM((EXTRA, rows), F32)),
        in_specs=[vmem] * 4,
        out_specs=(vmem,) * 2,
        compiler_params=pltpu.CompilerParams(vmem_limit_bytes=(4 + peers // 8) * MIB),
        name="sum",
    )(arrived, w_self, w_neigh, cotangent)
    output, packed, term = pl.pallas_call(
        node_kernel,
        out_shape=(
            pltpu.VMEM((rows, hidden), BF16),
            pltpu.VMEM((peers, rows // 4 + max(slab, 16), hidden), BF16),
            shape((rows, fin), F32),
        ),
        in_specs=[vmem] * 8,
        out_specs=(vmem,) * 3,
        scratch_shapes=[
            pltpu.VMEM((fin, rows), BF16),
            pltpu.VMEM((rows, fin), BF16),
            pltpu.VMEM((rows, hidden), F32),
            pltpu.VMEM((rows, hidden), BF16),
        ],
        compiler_params=pltpu.CompilerParams(vmem_limit_bytes=(4 + peers // 8) * MIB),
        name="node",
    )(total, swap(total), links, outside, features, w_self, w_neigh, cotangent)
    back = exchange(packed, middle)
    half_back = back[:, : rows // 4]
    pair = lax.ppermute(half_back, "dom", [(i, i ^ 1) for i in range(peers)])
    summed = pl.pallas_call(
        spread_kernel,
        out_shape=pltpu.VMEM((owners, slab, hidden), BF16),
        in_specs=[vmem],
        out_specs=vmem,
        compiler_params=pltpu.CompilerParams(vmem_limit_bytes=(4 + peers // 16) * MIB),
        name="spread",
    )(back)
    summed, half_back = lax.optimization_barrier((summed, half_back))
    weight = exchange(summed, corner)
    term = pl.pallas_call(
        input_kernel,
        out_shape=shape((rows, fin), F32),
        in_specs=[vmem] * 5,
        out_specs=vmem,
        scratch_shapes=[
            pltpu.SMEM((tile_count,), jnp.int32),
            pltpu.VMEM((peers, rows, fin), BF16),
            pltpu.SemaphoreType.DMA,
        ],
        compiler_params=pltpu.CompilerParams(vmem_limit_bytes=(4 + peers // 8) * MIB),
        name="input",
    )(targets, half_back, pair, tiles, term)
    block = shape((fin, hidden), F32)
    return pl.pallas_call(
        output_kernel,
        out_shape=(shape((rows, hidden), BF16), shape((rows, fin), BF16), block, block),
        in_specs=[vmem] * 4,
        out_specs=(vmem,) * 4,
        compiler_params=pltpu.CompilerParams(vmem_limit_bytes=4 * MIB),
        name="outputs",
    )(output, term, swap(term), weight.reshape(2 * fin, hidden))


def solution(mesh):
    placed = (
        P("dom", None),
        P(None, "feat"),
        P(None, "feat"),
        P("dom", None, None),
        P("dom", None),
        P("dom"),
        P("dom", "feat"),
    )
    return jax.shard_map(
        on_device,
        mesh=mesh,
        in_specs=placed,
        out_specs=(P("dom", "feat"), P("dom", None), P(None, "feat"), P(None, "feat")),
        check_vma=False,
    )
```

```python
import jax
import jax.numpy as jnp
from jax import lax
from jax.experimental import pallas as pl
from jax.experimental.pallas import tpu as pltpu
from jax.sharding import PartitionSpec as P

BF16 = jnp.bfloat16
F32 = jnp.float32
EXTRA = 8
SHARERS = 2
PAIR = 4
MIB = 1 << 20

NN = (((1,), (0,)), ((), ()))
NT = (((1,), (1,)), ((), ()))


def dot(a, b, dims):
    return lax.dot_general(a, b, dims, preferred_element_type=F32)


def loop(count, body):
    if count <= 16:
        for index in range(count):
            body(index)
    else:
        pl.loop(0, count)(body)


def listed(index, peers, corner=False):
    bits = peers.bit_length() - 1
    index = index ^ (peers - 1 if corner else peers - peers // 4 - 1)
    return sum(((index >> bit) & 1) << (bits - 1 - bit) for bit in range(bits))


def halves(size):
    core = lax.axis_index("feat")
    half = size // 2
    return pl.ds(pl.multiple_of(core * half, half), half), pl.ds(pl.multiple_of((1 - core) * half, half), half)


def share_kernel(
    dest_hbm, features_hbm, outside_hbm, tiles_hbm, share_ref, outside_ref, targets_ref, dest_ref, features_ref, tiles_ref, turned_ref, sums_ref, sems,
):
    copies = [
        pltpu.make_async_copy(source, target, sems.at[i])
        for i, (source, target) in enumerate(
            [
                (tiles_hbm, tiles_ref), (features_hbm, features_ref), (dest_hbm, dest_ref),
                (outside_hbm, outside_ref), (dest_hbm, targets_ref),
            ]
        )
    ]
    for copy in copies:
        copy.start()
    peers = sums_ref.shape[0]
    sums_ref[...] = jnp.zeros_like(sums_ref)
    copies[1].wait()
    turned_ref[...] = features_ref[...].T
    own, _ = halves(turned_ref.shape[0])
    left = jnp.concatenate([turned_ref[own, :], jnp.ones((EXTRA, turned_ref.shape[1]), BF16)], axis=0)
    copies[2].wait()
    copies[0].wait()

    def add(t):
        sums_ref[listed(dest_ref[t], peers)] += dot(left, tiles_ref[t], NN)

    loop(tiles_ref.shape[0], add)
    share_ref[...] = sums_ref[...].astype(BF16)
    copies[3].wait()
    copies[4].wait()


def sum_kernel(arrived_ref, w_self_ref, w_neigh_ref, cotangent_ref, total_ref, links_ref):
    half = arrived_ref.shape[1] - EXTRA
    fin = w_self_ref.shape[0]
    total = jnp.sum(arrived_ref[...].astype(F32), axis=0)
    links_ref[...] = total[half:]
    total_ref[:half] = total[:half].astype(BF16)
    total_ref[half : half + fin] = w_self_ref[...]
    total_ref[half + fin : half + 2 * fin] = w_neigh_ref[...]
    _, sibling = halves(cotangent_ref.shape[0])
    total_ref[half + 2 * fin :] = cotangent_ref[sibling, :]


def node_kernel(
    total_ref, other_ref, links_ref, outside_ref, features_ref, w_self_ref, w_neigh_ref, cotangent_ref,
    output_ref, packed_ref, term_ref, gathered_ref, nodes_ref, scale_ref, dagg_ref,
):
    fin, rows = gathered_ref.shape
    hidden = w_self_ref.shape[1]
    quarter = fin // 2
    own, sibling = halves(fin)
    low, _ = halves(rows)
    gathered_ref[own, :] = total_ref[:quarter]
    gathered_ref[sibling, :] = other_ref[:quarter]
    gathered = gathered_ref[...]
    nodes_ref[...] = gathered.T
    degree = links_ref[0:1] + outside_ref[...].astype(F32)
    scale_ref[...] = jnp.broadcast_to(1.0 / degree, (hidden, rows)).T

    def gradients(features, nodes, scale, w_self, w_neigh, cotangent):
        pre = dot(features, w_self, NN) + dot(nodes, w_neigh, NN) * scale
        sigma = 1.0 / (1.0 + jnp.exp(-pre))
        dpre = (cotangent.astype(F32) * sigma * (1.0 + pre * (1.0 - sigma))).astype(BF16)
        return pre * sigma, dpre, (dpre.astype(F32) * scale).astype(BF16)

    features, w_neigh = features_ref[...], w_neigh_ref[...]
    silu, dpre, dagg = gradients(
        features, nodes_ref[...], scale_ref[...], w_self_ref[...], w_neigh, cotangent_ref[...]
    )
    output_ref[...] = silu.astype(BF16)
    dagg_ref[...] = dagg
    w_self_other = other_ref[quarter : quarter + fin]
    w_neigh_other = other_ref[quarter + fin : quarter + 2 * fin]
    _, _, dagg_other = gradients(
        features_ref[low, :], nodes_ref[low, :], scale_ref[low, :], w_self_other, w_neigh_other,
        other_ref[quarter + 2 * fin :],
    )
    back = dot(dagg_ref[low, :], w_neigh, NT) + dot(dagg_other, w_neigh_other, NT)
    peers, packed, _ = packed_ref.shape
    owners = peers // SHARERS
    slab = 2 * fin // owners
    half = rows // 4
    back = back.astype(BF16)
    weight = jnp.concatenate([dot(features.T, dpre, NN), dot(gathered, dagg, NN)], axis=0)
    weight = weight.reshape(owners, slab, hidden)
    if packed - half > slab:
        weight = jnp.concatenate([weight, jnp.zeros((owners, packed - half - slab, hidden), F32)], axis=1)
    order = sorted(range(peers), key=lambda index: listed(index, peers))
    for k, index in enumerate(order):
        first = half if index & PAIR else 0
        packed_ref[k, :half] = back[first : first + half]
        packed_ref[k, half:] = weight[listed(index % owners, owners, corner=True)].astype(BF16)
    term_ref[...] = dot(dpre, w_self_ref[...], NT)


def input_kernel(targets_ref, back_ref, pair_ref, tiles_ref, term_ref, total_ref, dest_ref, padded_ref, sem):
    copy = pltpu.make_async_copy(targets_ref, dest_ref, sem)
    copy.start()
    half = tiles_ref.shape[2] // 2
    _, sibling = halves(tiles_ref.shape[2])
    quarter = half // 2
    first = lax.axis_index("feat") * half
    odd = (lax.axis_index("dom") // PAIR) & 1
    padded_ref[:, pl.ds(pl.multiple_of(first + odd * quarter, quarter), quarter), :] = back_ref[...]
    padded_ref[:, pl.ds(pl.multiple_of(first + (1 - odd) * quarter, quarter), quarter), :] = pair_ref[...]
    padded_ref[:, sibling, :] = jnp.zeros((padded_ref.shape[0], half, padded_ref.shape[2]), BF16)
    peers = padded_ref.shape[0]
    total = term_ref[...]
    copy.wait()
    if tiles_ref.shape[0] <= 16:
        for t in range(tiles_ref.shape[0]):
            total = total + dot(tiles_ref[t], padded_ref[listed(dest_ref[t], peers)], NN)
    else:
        total = lax.fori_loop(
            0, tiles_ref.shape[0], lambda t, sum: sum + dot(tiles_ref[t], padded_ref[listed(dest_ref[t], peers)], NN), total
        )
    total_ref[...] = total


def spread_kernel(back_ref, parts_ref):
    _, slab, _ = parts_ref.shape
    half = back_ref.shape[2] // 4
    part = jnp.sum(back_ref[:, half : half + slab].astype(F32), axis=0).astype(BF16)
    parts_ref[...] = jnp.broadcast_to(part[None], parts_ref.shape)


def output_kernel(silu_ref, term_ref, other_ref, weight_ref, output_ref, grad_input_ref, grad_self_ref, grad_neigh_ref):
    output_ref[...] = silu_ref[...]
    fin = grad_self_ref.shape[0]
    grad_input_ref[...] = (term_ref[...] + other_ref[...]).astype(BF16)
    grad_self_ref[...] = weight_ref[:fin].astype(F32)
    grad_neigh_ref[...] = weight_ref[fin:].astype(F32)


def on_device(features, w_self, w_neigh, tiles, dest, outside, cotangent):
    peers = lax.axis_size("dom")
    tile_count, rows, _ = tiles.shape
    fin, hidden = w_self.shape
    half = fin // 2
    slab = 2 * fin // (peers // SHARERS)
    vmem = pl.BlockSpec(memory_space=pltpu.VMEM)
    hbm = pl.BlockSpec(memory_space=pltpu.HBM)
    targets = dest.reshape(-1)
    shape = jax.ShapeDtypeStruct

    def swap(x):
        return lax.ppermute(x, "feat", [(0, 1), (1, 0)])

    def exchange(x, groups):
        return lax.all_to_all(x, "dom", split_axis=0, concat_axis=0, tiled=True, axis_index_groups=groups)

    middle = [sorted(range(peers), key=lambda index: listed(index, peers))]
    owners = peers // SHARERS
    corner = sorted(range(owners), key=lambda index: listed(index, owners, corner=True))
    corner = [[first + index for index in corner] for first in range(0, peers, owners)]
    extended = half + EXTRA
    share, outside, targets = pl.pallas_call(
        share_kernel,
        out_shape=(
            pltpu.VMEM((peers, extended, rows), BF16),
            pltpu.VMEM((1, rows), jnp.int32),
            pltpu.VMEM((tile_count,), jnp.int32),
        ),
        in_specs=[hbm] * 4,
        out_specs=(vmem,) * 3,
        scratch_shapes=[
            pltpu.SMEM((tile_count,), jnp.int32),
            pltpu.VMEM((rows, fin), BF16),
            pltpu.VMEM(tiles.shape, BF16),
            pltpu.VMEM((fin, rows), BF16),
            pltpu.VMEM((peers, extended, rows), F32),
            pltpu.SemaphoreType.DMA((5,)),
        ],
        compiler_params=pltpu.CompilerParams(vmem_limit_bytes=60 * MIB),
        name="share",
    )(targets, features, outside.reshape(1, rows), tiles)
    arrived = exchange(share, middle)
    together = half + 2 * fin + rows // 2
    total, links = pl.pallas_call(
        sum_kernel,
        out_shape=(pltpu.VMEM((together, hidden), BF16), pltpu.VMEM((EXTRA, rows), F32)),
        in_specs=[vmem] * 4,
        out_specs=(vmem,) * 2,
        compiler_params=pltpu.CompilerParams(vmem_limit_bytes=(4 + peers // 8) * MIB),
        name="sum",
    )(arrived, w_self, w_neigh, cotangent)
    output, packed, term = pl.pallas_call(
        node_kernel,
        out_shape=(
            pltpu.VMEM((rows, hidden), BF16),
            pltpu.VMEM((peers, rows // 4 + max(slab, 16), hidden), BF16),
            shape((rows, fin), F32),
        ),
        in_specs=[vmem] * 8,
        out_specs=(vmem,) * 3,
        scratch_shapes=[
            pltpu.VMEM((fin, rows), BF16),
            pltpu.VMEM((rows, fin), BF16),
            pltpu.VMEM((rows, hidden), F32),
            pltpu.VMEM((rows, hidden), BF16),
        ],
        compiler_params=pltpu.CompilerParams(vmem_limit_bytes=(4 + peers // 8) * MIB),
        name="node",
    )(total, swap(total), links, outside, features, w_self, w_neigh, cotangent)
    back = exchange(packed, middle)
    half_back = back[:, : rows // 4]
    pair = lax.ppermute(half_back, "dom", [(i, i ^ PAIR) for i in range(peers)])
    summed = pl.pallas_call(
        spread_kernel,
        out_shape=pltpu.VMEM((owners, slab, hidden), BF16),
        in_specs=[vmem],
        out_specs=vmem,
        compiler_params=pltpu.CompilerParams(vmem_limit_bytes=(4 + peers // 16) * MIB),
        name="spread",
    )(back)
    summed, half_back = lax.optimization_barrier((summed, half_back))
    weight = exchange(summed, corner)
    term = pl.pallas_call(
        input_kernel,
        out_shape=shape((rows, fin), F32),
        in_specs=[vmem] * 5,
        out_specs=vmem,
        scratch_shapes=[
            pltpu.SMEM((tile_count,), jnp.int32),
            pltpu.VMEM((peers, rows, fin), BF16),
            pltpu.SemaphoreType.DMA,
        ],
        compiler_params=pltpu.CompilerParams(vmem_limit_bytes=(4 + peers // 8) * MIB),
        name="input",
    )(targets, half_back, pair, tiles, term)
    block = shape((fin, hidden), F32)
    return pl.pallas_call(
        output_kernel,
        out_shape=(shape((rows, hidden), BF16), shape((rows, fin), BF16), block, block),
        in_specs=[vmem] * 4,
        out_specs=(vmem,) * 4,
        compiler_params=pltpu.CompilerParams(vmem_limit_bytes=4 * MIB),
        name="outputs",
    )(output, term, swap(term), weight.reshape(2 * fin, hidden))


def solution(mesh):
    placed = (
        P("dom", None),
        P(None, "feat"),
        P(None, "feat"),
        P("dom", None, None),
        P("dom", None),
        P("dom"),
        P("dom", "feat"),
    )
    return jax.shard_map(
        on_device,
        mesh=mesh,
        in_specs=placed,
        out_specs=(P("dom", "feat"), P("dom", None), P(None, "feat"), P(None, "feat")),
        check_vma=False,
    )
```

```python
import jax
import jax.numpy as jnp
from jax import lax
from jax.experimental import pallas as pl
from jax.experimental.pallas import tpu as pltpu
from jax.sharding import PartitionSpec as P

BF16 = jnp.bfloat16
F32 = jnp.float32
EXTRA = 8
SHARERS = 2
PAIR = 4
MIB = 1 << 20

NN = (((1,), (0,)), ((), ()))
NT = (((1,), (1,)), ((), ()))


def dot(a, b, dims):
    return lax.dot_general(a, b, dims, preferred_element_type=F32)


def loop(count, body):
    if count <= 16:
        for index in range(count):
            body(index)
    else:
        pl.loop(0, count)(body)


def listed(index, peers, corner=False):
    bits = peers.bit_length() - 1
    index = index ^ (peers - 1 if corner else peers - peers // 4 - 1)
    return sum(((index >> bit) & 1) << (bits - 1 - bit) for bit in range(bits))


def halves(size):
    core = lax.axis_index("feat")
    half = size // 2
    return pl.ds(pl.multiple_of(core * half, half), half), pl.ds(pl.multiple_of((1 - core) * half, half), half)


def share_kernel(
    dest_hbm, features_hbm, outside_hbm, tiles_hbm, share_ref, outside_ref, targets_ref, dest_ref, features_ref, tiles_ref, turned_ref, sums_ref, sems,
):
    copies = [
        pltpu.make_async_copy(source, target, sems.at[i])
        for i, (source, target) in enumerate(
            [
                (tiles_hbm, tiles_ref), (features_hbm, features_ref), (dest_hbm, dest_ref),
                (outside_hbm, outside_ref), (dest_hbm, targets_ref),
            ]
        )
    ]
    for copy in copies:
        copy.start()
    peers = sums_ref.shape[0]
    sums_ref[...] = jnp.zeros_like(sums_ref)
    copies[1].wait()
    turned_ref[...] = features_ref[...].T
    own, _ = halves(turned_ref.shape[0])
    left = jnp.concatenate([turned_ref[own, :], jnp.ones((EXTRA, turned_ref.shape[1]), BF16)], axis=0)
    copies[2].wait()
    copies[0].wait()

    def add(t):
        sums_ref[listed(dest_ref[t], peers)] += dot(left, tiles_ref[t], NN)

    loop(tiles_ref.shape[0], add)
    share_ref[...] = sums_ref[...].astype(BF16)
    copies[3].wait()
    copies[4].wait()


def sum_kernel(arrived_ref, w_self_ref, w_neigh_ref, cotangent_ref, total_ref, links_ref):
    half = arrived_ref.shape[1] - EXTRA
    fin = w_self_ref.shape[0]
    total = jnp.sum(arrived_ref[...].astype(F32), axis=0)
    links_ref[...] = total[half:]
    total_ref[:half] = total[:half].astype(BF16)
    total_ref[half : half + fin] = w_self_ref[...]
    total_ref[half + fin : half + 2 * fin] = w_neigh_ref[...]
    _, sibling = halves(cotangent_ref.shape[0])
    total_ref[half + 2 * fin :] = cotangent_ref[sibling, :]


def node_kernel(
    total_ref, other_ref, links_ref, outside_ref, features_ref, w_self_ref, w_neigh_ref, cotangent_ref,
    output_ref, packed_ref, dpre_ref, gathered_ref, nodes_ref, scale_ref, dagg_ref,
):
    fin, rows = gathered_ref.shape
    hidden = w_self_ref.shape[1]
    quarter = fin // 2
    own, sibling = halves(fin)
    low, _ = halves(rows)
    gathered_ref[own, :] = total_ref[:quarter]
    gathered_ref[sibling, :] = other_ref[:quarter]
    gathered = gathered_ref[...]
    nodes_ref[...] = gathered.T
    degree = links_ref[0:1] + outside_ref[...].astype(F32)
    scale_ref[...] = jnp.broadcast_to(1.0 / degree, (hidden, rows)).T

    def gradients(features, nodes, scale, w_self, w_neigh, cotangent):
        pre = dot(features, w_self, NN) + dot(nodes, w_neigh, NN) * scale
        sigma = 1.0 / (1.0 + jnp.exp(-pre))
        dpre = (cotangent.astype(F32) * sigma * (1.0 + pre * (1.0 - sigma))).astype(BF16)
        return pre * sigma, dpre, (dpre.astype(F32) * scale).astype(BF16)

    features, w_neigh = features_ref[...], w_neigh_ref[...]
    silu, dpre, dagg = gradients(
        features, nodes_ref[...], scale_ref[...], w_self_ref[...], w_neigh, cotangent_ref[...]
    )
    output_ref[...] = silu.astype(BF16)
    dagg_ref[...] = dagg
    w_self_other = other_ref[quarter : quarter + fin]
    w_neigh_other = other_ref[quarter + fin : quarter + 2 * fin]
    _, _, dagg_other = gradients(
        features_ref[low, :], nodes_ref[low, :], scale_ref[low, :], w_self_other, w_neigh_other,
        other_ref[quarter + 2 * fin :],
    )
    back = dot(dagg_ref[low, :], w_neigh, NT) + dot(dagg_other, w_neigh_other, NT)
    peers, packed, _ = packed_ref.shape
    owners = peers // SHARERS
    slab = 2 * fin // owners
    half = rows // 4
    back = back.astype(BF16)
    weight = jnp.concatenate([dot(features.T, dpre, NN), dot(gathered, dagg, NN)], axis=0)
    weight = weight.reshape(owners, slab, hidden)
    if packed - half > slab:
        weight = jnp.concatenate([weight, jnp.zeros((owners, packed - half - slab, hidden), F32)], axis=1)
    order = sorted(range(peers), key=lambda index: listed(index, peers))
    for k, index in enumerate(order):
        first = half if index & PAIR else 0
        packed_ref[k, :half] = back[first : first + half]
        packed_ref[k, half:] = weight[listed(index % owners, owners, corner=True)].astype(BF16)
    dpre_ref[...] = dpre


def input_kernel(targets_ref, back_ref, pair_ref, tiles_ref, dpre_ref, w_self_ref, total_ref, dest_ref, padded_ref, sem):
    copy = pltpu.make_async_copy(targets_ref, dest_ref, sem)
    copy.start()
    half = tiles_ref.shape[2] // 2
    _, sibling = halves(tiles_ref.shape[2])
    quarter = half // 2
    first = lax.axis_index("feat") * half
    odd = (lax.axis_index("dom") // PAIR) & 1
    padded_ref[:, pl.ds(pl.multiple_of(first + odd * quarter, quarter), quarter), :] = back_ref[...]
    padded_ref[:, pl.ds(pl.multiple_of(first + (1 - odd) * quarter, quarter), quarter), :] = pair_ref[...]
    padded_ref[:, sibling, :] = jnp.zeros((padded_ref.shape[0], half, padded_ref.shape[2]), BF16)
    peers = padded_ref.shape[0]
    total = dot(dpre_ref[...], w_self_ref[...], NT)
    copy.wait()
    if tiles_ref.shape[0] <= 16:
        for t in range(tiles_ref.shape[0]):
            total = total + dot(tiles_ref[t], padded_ref[listed(dest_ref[t], peers)], NN)
    else:
        total = lax.fori_loop(
            0, tiles_ref.shape[0], lambda t, sum: sum + dot(tiles_ref[t], padded_ref[listed(dest_ref[t], peers)], NN), total
        )
    total_ref[...] = total


def spread_kernel(back_ref, parts_ref):
    _, slab, _ = parts_ref.shape
    half = back_ref.shape[2] // 4
    part = jnp.sum(back_ref[:, half : half + slab].astype(F32), axis=0).astype(BF16)
    parts_ref[...] = jnp.broadcast_to(part[None], parts_ref.shape)


def output_kernel(silu_ref, term_ref, other_ref, weight_ref, output_ref, grad_input_ref, grad_self_ref, grad_neigh_ref):
    output_ref[...] = silu_ref[...]
    fin = grad_self_ref.shape[0]
    grad_input_ref[...] = (term_ref[...] + other_ref[...]).astype(BF16)
    grad_self_ref[...] = weight_ref[:fin].astype(F32)
    grad_neigh_ref[...] = weight_ref[fin:].astype(F32)


def on_device(features, w_self, w_neigh, tiles, dest, outside, cotangent):
    peers = lax.axis_size("dom")
    tile_count, rows, _ = tiles.shape
    fin, hidden = w_self.shape
    half = fin // 2
    slab = 2 * fin // (peers // SHARERS)
    vmem = pl.BlockSpec(memory_space=pltpu.VMEM)
    hbm = pl.BlockSpec(memory_space=pltpu.HBM)
    targets = dest.reshape(-1)
    shape = jax.ShapeDtypeStruct

    def swap(x):
        return lax.ppermute(x, "feat", [(0, 1), (1, 0)])

    def exchange(x, groups):
        return lax.all_to_all(x, "dom", split_axis=0, concat_axis=0, tiled=True, axis_index_groups=groups)

    middle = [sorted(range(peers), key=lambda index: listed(index, peers))]
    owners = peers // SHARERS
    corner = sorted(range(owners), key=lambda index: listed(index, owners, corner=True))
    corner = [[first + index for index in corner] for first in range(0, peers, owners)]
    extended = half + EXTRA
    share, outside, targets = pl.pallas_call(
        share_kernel,
        out_shape=(
            pltpu.VMEM((peers, extended, rows), BF16),
            pltpu.VMEM((1, rows), jnp.int32),
            pltpu.VMEM((tile_count,), jnp.int32),
        ),
        in_specs=[hbm] * 4,
        out_specs=(vmem,) * 3,
        scratch_shapes=[
            pltpu.SMEM((tile_count,), jnp.int32),
            pltpu.VMEM((rows, fin), BF16),
            pltpu.VMEM(tiles.shape, BF16),
            pltpu.VMEM((fin, rows), BF16),
            pltpu.VMEM((peers, extended, rows), F32),
            pltpu.SemaphoreType.DMA((5,)),
        ],
        compiler_params=pltpu.CompilerParams(vmem_limit_bytes=60 * MIB),
        name="share",
    )(targets, features, outside.reshape(1, rows), tiles)
    arrived = exchange(share, middle)
    together = half + 2 * fin + rows // 2
    total, links = pl.pallas_call(
        sum_kernel,
        out_shape=(pltpu.VMEM((together, hidden), BF16), pltpu.VMEM((EXTRA, rows), F32)),
        in_specs=[vmem] * 4,
        out_specs=(vmem,) * 2,
        compiler_params=pltpu.CompilerParams(vmem_limit_bytes=(4 + peers // 8) * MIB),
        name="sum",
    )(arrived, w_self, w_neigh, cotangent)
    output, packed, dpre = pl.pallas_call(
        node_kernel,
        out_shape=(
            pltpu.VMEM((rows, hidden), BF16),
            pltpu.VMEM((peers, rows // 4 + max(slab, 16), hidden), BF16),
            pltpu.VMEM((rows, hidden), BF16),
        ),
        in_specs=[vmem] * 8,
        out_specs=(vmem,) * 3,
        scratch_shapes=[
            pltpu.VMEM((fin, rows), BF16),
            pltpu.VMEM((rows, fin), BF16),
            pltpu.VMEM((rows, hidden), F32),
            pltpu.VMEM((rows, hidden), BF16),
        ],
        compiler_params=pltpu.CompilerParams(vmem_limit_bytes=(4 + peers // 8) * MIB),
        name="node",
    )(total, swap(total), links, outside, features, w_self, w_neigh, cotangent)
    back = exchange(packed, middle)
    half_back = back[:, : rows // 4]
    pair = lax.ppermute(half_back, "dom", [(i, i ^ PAIR) for i in range(peers)])
    summed = pl.pallas_call(
        spread_kernel,
        out_shape=pltpu.VMEM((owners, slab, hidden), BF16),
        in_specs=[vmem],
        out_specs=vmem,
        compiler_params=pltpu.CompilerParams(vmem_limit_bytes=(4 + peers // 16) * MIB),
        name="spread",
    )(back)
    summed, half_back = lax.optimization_barrier((summed, half_back))
    weight = exchange(summed, corner)
    term = pl.pallas_call(
        input_kernel,
        out_shape=shape((rows, fin), F32),
        in_specs=[vmem] * 6,
        out_specs=vmem,
        scratch_shapes=[
            pltpu.SMEM((tile_count,), jnp.int32),
            pltpu.VMEM((peers, rows, fin), BF16),
            pltpu.SemaphoreType.DMA,
        ],
        compiler_params=pltpu.CompilerParams(vmem_limit_bytes=(4 + peers // 8) * MIB),
        name="input",
    )(targets, half_back, pair, tiles, dpre, w_self)
    block = shape((fin, hidden), F32)
    return pl.pallas_call(
        output_kernel,
        out_shape=(shape((rows, hidden), BF16), shape((rows, fin), BF16), block, block),
        in_specs=[vmem] * 4,
        out_specs=(vmem,) * 4,
        compiler_params=pltpu.CompilerParams(vmem_limit_bytes=4 * MIB),
        name="outputs",
    )(output, term, swap(term), weight.reshape(2 * fin, hidden))


def solution(mesh):
    placed = (
        P("dom", None),
        P(None, "feat"),
        P(None, "feat"),
        P("dom", None, None),
        P("dom", None),
        P("dom"),
        P("dom", "feat"),
    )
    return jax.shard_map(
        on_device,
        mesh=mesh,
        in_specs=placed,
        out_specs=(P("dom", "feat"), P("dom", None), P(None, "feat"), P(None, "feat")),
        check_vma=False,
    )
```

```python
import jax
import jax.numpy as jnp
from jax import lax
from jax.experimental import pallas as pl
from jax.experimental.pallas import tpu as pltpu
from jax.sharding import PartitionSpec as P

BF16 = jnp.bfloat16
F32 = jnp.float32
EXTRA = 8
SHARERS = 2
PAIR = 4
MIB = 1 << 20

NN = (((1,), (0,)), ((), ()))
NT = (((1,), (1,)), ((), ()))


def dot(a, b, dims):
    return lax.dot_general(a, b, dims, preferred_element_type=F32)


def loop(count, body):
    if count <= 16:
        for index in range(count):
            body(index)
    else:
        pl.loop(0, count)(body)


def listed(index, peers, corner=False):
    bits = peers.bit_length() - 1
    index = index ^ (peers - 1 if corner else peers - peers // 4 - 1)
    return sum(((index >> bit) & 1) << (bits - 1 - bit) for bit in range(bits))


def halves(size):
    core = lax.axis_index("feat")
    half = size // 2
    return pl.ds(pl.multiple_of(core * half, half), half), pl.ds(pl.multiple_of((1 - core) * half, half), half)


def share_kernel(
    dest_hbm, features_hbm, outside_hbm, tiles_hbm, share_ref, outside_ref, targets_ref, dest_ref, features_ref, tiles_ref, turned_ref, sums_ref, sems,
):
    copies = [
        pltpu.make_async_copy(source, target, sems.at[i])
        for i, (source, target) in enumerate(
            [
                (tiles_hbm, tiles_ref), (features_hbm, features_ref), (dest_hbm, dest_ref),
                (outside_hbm, outside_ref), (dest_hbm, targets_ref),
            ]
        )
    ]
    for copy in copies:
        copy.start()
    peers = sums_ref.shape[0]
    sums_ref[...] = jnp.zeros_like(sums_ref)
    copies[1].wait()
    turned_ref[...] = features_ref[...].T
    own, _ = halves(turned_ref.shape[0])
    left = jnp.concatenate([turned_ref[own, :], jnp.ones((EXTRA, turned_ref.shape[1]), BF16)], axis=0)
    copies[2].wait()
    copies[0].wait()

    def add(t):
        sums_ref[listed(dest_ref[t], peers)] += dot(left, tiles_ref[t], NN)

    loop(tiles_ref.shape[0], add)
    share_ref[...] = sums_ref[...].astype(BF16)
    copies[3].wait()
    copies[4].wait()


def sum_kernel(arrived_ref, w_self_ref, w_neigh_ref, cotangent_ref, total_ref, links_ref):
    half = arrived_ref.shape[1] - EXTRA
    fin = w_self_ref.shape[0]
    total = jnp.sum(arrived_ref[...].astype(F32), axis=0)
    links_ref[...] = total[half:]
    total_ref[:half] = total[:half].astype(BF16)
    total_ref[half : half + fin] = w_self_ref[...]
    total_ref[half + fin : half + 2 * fin] = w_neigh_ref[...]
    _, sibling = halves(cotangent_ref.shape[0])
    total_ref[half + 2 * fin :] = cotangent_ref[sibling, :]


def node_kernel(
    total_ref, other_ref, links_ref, outside_ref, features_ref, w_self_ref, w_neigh_ref, cotangent_ref,
    output_ref, packed_ref, dpre_ref, gathered_ref, nodes_ref, scale_ref, dagg_ref,
):
    fin, rows = gathered_ref.shape
    hidden = w_self_ref.shape[1]
    quarter = fin // 2
    own, sibling = halves(fin)
    low, _ = halves(rows)
    gathered_ref[own, :] = total_ref[:quarter]
    gathered_ref[sibling, :] = other_ref[:quarter]
    gathered = gathered_ref[...]
    nodes_ref[...] = gathered.T
    degree = links_ref[0:1] + outside_ref[...].astype(F32)
    scale_ref[...] = jnp.broadcast_to(1.0 / degree, (hidden, rows)).T

    def gradients(features, nodes, scale, w_self, w_neigh, cotangent):
        pre = dot(features, w_self, NN) + dot(nodes, w_neigh, NN) * scale
        sigma = 1.0 / (1.0 + jnp.exp(-pre))
        dpre = (cotangent.astype(F32) * sigma * (1.0 + pre * (1.0 - sigma))).astype(BF16)
        return pre * sigma, dpre, (dpre.astype(F32) * scale).astype(BF16)

    features, w_neigh = features_ref[...], w_neigh_ref[...]
    silu, dpre, dagg = gradients(
        features, nodes_ref[...], scale_ref[...], w_self_ref[...], w_neigh, cotangent_ref[...]
    )
    output_ref[...] = silu.astype(BF16)
    dagg_ref[...] = dagg
    w_self_other = other_ref[quarter : quarter + fin]
    w_neigh_other = other_ref[quarter + fin : quarter + 2 * fin]
    _, _, dagg_other = gradients(
        features_ref[low, :], nodes_ref[low, :], scale_ref[low, :], w_self_other, w_neigh_other,
        other_ref[quarter + 2 * fin :],
    )
    back = dot(dagg_ref[low, :], w_neigh, NT) + dot(dagg_other, w_neigh_other, NT)
    peers, packed, _ = packed_ref.shape
    owners = peers // SHARERS
    slab = 2 * fin // owners
    half = rows // 4
    back = back.astype(BF16)
    weight = jnp.concatenate([dot(features.T, dpre, NN), dot(gathered, dagg, NN)], axis=0)
    weight = weight.reshape(owners, slab, hidden)
    if packed - half > slab:
        weight = jnp.concatenate([weight, jnp.zeros((owners, packed - half - slab, hidden), F32)], axis=1)
    order = sorted(range(peers), key=lambda index: listed(index, peers))
    for k, index in enumerate(order):
        first = half if index & PAIR else 0
        packed_ref[k, :half] = back[first : first + half]
        packed_ref[k, half:] = weight[listed(index % owners, owners, corner=True)].astype(BF16)
    dpre_ref[...] = dpre


def input_kernel(
    targets_ref, back_ref, pair_ref, tiles_ref, dpre_ref, w_self_ref, silu_ref, total_ref, output_hbm, dest_ref, padded_ref, sems,
):
    copy = pltpu.make_async_copy(targets_ref, dest_ref, sems.at[0])
    write = pltpu.make_async_copy(silu_ref, output_hbm, sems.at[1])
    copy.start()
    write.start()
    half = tiles_ref.shape[2] // 2
    _, sibling = halves(tiles_ref.shape[2])
    quarter = half // 2
    first = lax.axis_index("feat") * half
    odd = (lax.axis_index("dom") // PAIR) & 1
    padded_ref[:, pl.ds(pl.multiple_of(first + odd * quarter, quarter), quarter), :] = back_ref[...]
    padded_ref[:, pl.ds(pl.multiple_of(first + (1 - odd) * quarter, quarter), quarter), :] = pair_ref[...]
    padded_ref[:, sibling, :] = jnp.zeros((padded_ref.shape[0], half, padded_ref.shape[2]), BF16)
    peers = padded_ref.shape[0]
    total = dot(dpre_ref[...], w_self_ref[...], NT)
    copy.wait()
    if tiles_ref.shape[0] <= 16:
        for t in range(tiles_ref.shape[0]):
            total = total + dot(tiles_ref[t], padded_ref[listed(dest_ref[t], peers)], NN)
    else:
        total = lax.fori_loop(
            0, tiles_ref.shape[0], lambda t, sum: sum + dot(tiles_ref[t], padded_ref[listed(dest_ref[t], peers)], NN), total
        )
    total_ref[...] = total
    write.wait()


def spread_kernel(back_ref, parts_ref):
    _, slab, _ = parts_ref.shape
    half = back_ref.shape[2] // 4
    part = jnp.sum(back_ref[:, half : half + slab].astype(F32), axis=0).astype(BF16)
    parts_ref[...] = jnp.broadcast_to(part[None], parts_ref.shape)


def output_kernel(term_ref, other_ref, weight_ref, grad_input_ref, grad_self_ref, grad_neigh_ref):
    fin = grad_self_ref.shape[0]
    grad_input_ref[...] = (term_ref[...] + other_ref[...]).astype(BF16)
    grad_self_ref[...] = weight_ref[:fin].astype(F32)
    grad_neigh_ref[...] = weight_ref[fin:].astype(F32)


def on_device(features, w_self, w_neigh, tiles, dest, outside, cotangent):
    peers = lax.axis_size("dom")
    tile_count, rows, _ = tiles.shape
    fin, hidden = w_self.shape
    half = fin // 2
    slab = 2 * fin // (peers // SHARERS)
    vmem = pl.BlockSpec(memory_space=pltpu.VMEM)
    hbm = pl.BlockSpec(memory_space=pltpu.HBM)
    targets = dest.reshape(-1)
    shape = jax.ShapeDtypeStruct

    def swap(x):
        return lax.ppermute(x, "feat", [(0, 1), (1, 0)])

    def exchange(x, groups):
        return lax.all_to_all(x, "dom", split_axis=0, concat_axis=0, tiled=True, axis_index_groups=groups)

    middle = [sorted(range(peers), key=lambda index: listed(index, peers))]
    owners = peers // SHARERS
    corner = sorted(range(owners), key=lambda index: listed(index, owners, corner=True))
    corner = [[first + index for index in corner] for first in range(0, peers, owners)]
    extended = half + EXTRA
    share, outside, targets = pl.pallas_call(
        share_kernel,
        out_shape=(
            pltpu.VMEM((peers, extended, rows), BF16),
            pltpu.VMEM((1, rows), jnp.int32),
            pltpu.VMEM((tile_count,), jnp.int32),
        ),
        in_specs=[hbm] * 4,
        out_specs=(vmem,) * 3,
        scratch_shapes=[
            pltpu.SMEM((tile_count,), jnp.int32),
            pltpu.VMEM((rows, fin), BF16),
            pltpu.VMEM(tiles.shape, BF16),
            pltpu.VMEM((fin, rows), BF16),
            pltpu.VMEM((peers, extended, rows), F32),
            pltpu.SemaphoreType.DMA((5,)),
        ],
        compiler_params=pltpu.CompilerParams(vmem_limit_bytes=60 * MIB),
        name="share",
    )(targets, features, outside.reshape(1, rows), tiles)
    arrived = exchange(share, middle)
    together = half + 2 * fin + rows // 2
    total, links = pl.pallas_call(
        sum_kernel,
        out_shape=(pltpu.VMEM((together, hidden), BF16), pltpu.VMEM((EXTRA, rows), F32)),
        in_specs=[vmem] * 4,
        out_specs=(vmem,) * 2,
        compiler_params=pltpu.CompilerParams(vmem_limit_bytes=(4 + peers // 8) * MIB),
        name="sum",
    )(arrived, w_self, w_neigh, cotangent)
    output, packed, dpre = pl.pallas_call(
        node_kernel,
        out_shape=(
            pltpu.VMEM((rows, hidden), BF16),
            pltpu.VMEM((peers, rows // 4 + max(slab, 16), hidden), BF16),
            pltpu.VMEM((rows, hidden), BF16),
        ),
        in_specs=[vmem] * 8,
        out_specs=(vmem,) * 3,
        scratch_shapes=[
            pltpu.VMEM((fin, rows), BF16),
            pltpu.VMEM((rows, fin), BF16),
            pltpu.VMEM((rows, hidden), F32),
            pltpu.VMEM((rows, hidden), BF16),
        ],
        compiler_params=pltpu.CompilerParams(vmem_limit_bytes=(4 + peers // 8) * MIB),
        name="node",
    )(total, swap(total), links, outside, features, w_self, w_neigh, cotangent)
    back = exchange(packed, middle)
    half_back = back[:, : rows // 4]
    pair = lax.ppermute(half_back, "dom", [(i, i ^ PAIR) for i in range(peers)])
    summed = pl.pallas_call(
        spread_kernel,
        out_shape=pltpu.VMEM((owners, slab, hidden), BF16),
        in_specs=[vmem],
        out_specs=vmem,
        compiler_params=pltpu.CompilerParams(vmem_limit_bytes=(4 + peers // 16) * MIB),
        name="spread",
    )(back)
    summed, half_back = lax.optimization_barrier((summed, half_back))
    weight = exchange(summed, corner)
    term, output = pl.pallas_call(
        input_kernel,
        out_shape=(shape((rows, fin), F32), shape((rows, hidden), BF16)),
        in_specs=[vmem] * 7,
        out_specs=(vmem, hbm),
        scratch_shapes=[
            pltpu.SMEM((tile_count,), jnp.int32),
            pltpu.VMEM((peers, rows, fin), BF16),
            pltpu.SemaphoreType.DMA((2,)),
        ],
        compiler_params=pltpu.CompilerParams(vmem_limit_bytes=(4 + peers // 8) * MIB),
        name="input",
    )(targets, half_back, pair, tiles, dpre, w_self, output)
    block = shape((fin, hidden), F32)
    gradients = pl.pallas_call(
        output_kernel,
        out_shape=(shape((rows, fin), BF16), block, block),
        in_specs=[vmem] * 3,
        out_specs=(vmem,) * 3,
        compiler_params=pltpu.CompilerParams(vmem_limit_bytes=4 * MIB),
        name="outputs",
    )(term, swap(term), weight.reshape(2 * fin, hidden))
    return output, *gradients


def solution(mesh):
    placed = (
        P("dom", None),
        P(None, "feat"),
        P(None, "feat"),
        P("dom", None, None),
        P("dom", None),
        P("dom"),
        P("dom", "feat"),
    )
    return jax.shard_map(
        on_device,
        mesh=mesh,
        in_specs=placed,
        out_specs=(P("dom", "feat"), P("dom", None), P(None, "feat"), P(None, "feat")),
        check_vma=False,
    )
```

```python
import jax
import jax.numpy as jnp
from jax import lax
from jax.experimental import pallas as pl
from jax.experimental.pallas import tpu as pltpu
from jax.sharding import PartitionSpec as P

BF16 = jnp.bfloat16
F32 = jnp.float32
EXTRA = 8
SHARERS = 2
PAIR = 4
MIB = 1 << 20

NN = (((1,), (0,)), ((), ()))
NT = (((1,), (1,)), ((), ()))


def dot(a, b, dims):
    return lax.dot_general(a, b, dims, preferred_element_type=F32)


def loop(count, body):
    if count <= 16:
        for index in range(count):
            body(index)
    else:
        pl.loop(0, count)(body)


def listed(index, peers, corner=False):
    bits = peers.bit_length() - 1
    index = index ^ (peers - 1 if corner else peers - peers // 4 - 1)
    return sum(((index >> bit) & 1) << (bits - 1 - bit) for bit in range(bits))


def halves(size):
    core = lax.axis_index("feat")
    half = size // 2
    return pl.ds(pl.multiple_of(core * half, half), half), pl.ds(pl.multiple_of((1 - core) * half, half), half)


def share_kernel(
    dest_hbm, features_hbm, outside_hbm, tiles_hbm, share_ref, outside_ref, targets_ref, dest_ref, features_ref, tiles_ref, turned_ref, sums_ref, sems,
):
    copies = [
        pltpu.make_async_copy(source, target, sems.at[i])
        for i, (source, target) in enumerate(
            [
                (tiles_hbm, tiles_ref), (features_hbm, features_ref), (dest_hbm, dest_ref),
                (outside_hbm, outside_ref), (dest_hbm, targets_ref),
            ]
        )
    ]
    for copy in copies:
        copy.start()
    peers = sums_ref.shape[0]
    sums_ref[...] = jnp.zeros_like(sums_ref)
    copies[1].wait()
    turned_ref[...] = features_ref[...].T
    own, _ = halves(turned_ref.shape[0])
    left = jnp.concatenate([turned_ref[own, :], jnp.ones((EXTRA, turned_ref.shape[1]), BF16)], axis=0)
    copies[2].wait()
    copies[0].wait()

    def add(t):
        sums_ref[listed(dest_ref[t], peers)] += dot(left, tiles_ref[t], NN)

    loop(tiles_ref.shape[0], add)
    share_ref[...] = sums_ref[...].astype(BF16)
    copies[3].wait()
    copies[4].wait()


def sum_kernel(arrived_ref, w_self_ref, w_neigh_ref, cotangent_ref, total_ref, links_ref):
    half = arrived_ref.shape[1] - EXTRA
    fin = w_self_ref.shape[0]
    total = jnp.sum(arrived_ref[...].astype(F32), axis=0)
    links_ref[...] = total[half:]
    total_ref[:half] = total[:half].astype(BF16)
    total_ref[half : half + fin] = w_self_ref[...]
    total_ref[half + fin : half + 2 * fin] = w_neigh_ref[...]
    _, sibling = halves(cotangent_ref.shape[0])
    total_ref[half + 2 * fin :] = cotangent_ref[sibling, :]


def node_kernel(
    total_ref, other_ref, links_ref, outside_ref, features_ref, w_self_ref, w_neigh_ref, cotangent_ref,
    output_ref, packed_ref, dpre_ref, gathered_ref, nodes_ref, scale_ref, dagg_ref,
):
    fin, rows = gathered_ref.shape
    hidden = w_self_ref.shape[1]
    quarter = fin // 2
    own, sibling = halves(fin)
    low, _ = halves(rows)
    gathered_ref[own, :] = total_ref[:quarter]
    gathered_ref[sibling, :] = other_ref[:quarter]
    gathered = gathered_ref[...]
    nodes_ref[...] = gathered.T
    degree = links_ref[0:1] + outside_ref[...].astype(F32)
    scale_ref[...] = jnp.broadcast_to(1.0 / degree, (hidden, rows)).T

    def gradients(features, nodes, scale, w_self, w_neigh, cotangent):
        pre = dot(features, w_self, NN) + dot(nodes, w_neigh, NN) * scale
        sigma = 1.0 / (1.0 + jnp.exp(-pre))
        dpre = (cotangent.astype(F32) * sigma * (1.0 + pre * (1.0 - sigma))).astype(BF16)
        return pre * sigma, dpre, (dpre.astype(F32) * scale).astype(BF16)

    features, w_neigh = features_ref[...], w_neigh_ref[...]
    silu, dpre, dagg = gradients(
        features, nodes_ref[...], scale_ref[...], w_self_ref[...], w_neigh, cotangent_ref[...]
    )
    output_ref[...] = silu.astype(BF16)
    dagg_ref[...] = dagg
    w_self_other = other_ref[quarter : quarter + fin]
    w_neigh_other = other_ref[quarter + fin : quarter + 2 * fin]
    _, _, dagg_other = gradients(
        features_ref[low, :], nodes_ref[low, :], scale_ref[low, :], w_self_other, w_neigh_other,
        other_ref[quarter + 2 * fin :],
    )
    back = dot(dagg_ref[low, :], w_neigh, NT) + dot(dagg_other, w_neigh_other, NT)
    peers, packed, _ = packed_ref.shape
    owners = peers // SHARERS
    slab = 2 * fin // owners
    half = rows // 4
    back = back.astype(BF16)
    weight = jnp.concatenate([dot(features.T, dpre, NN), dot(gathered, dagg, NN)], axis=0)
    weight = weight.reshape(owners, slab, hidden)
    if packed - half > slab:
        weight = jnp.concatenate([weight, jnp.zeros((owners, packed - half - slab, hidden), F32)], axis=1)
    order = sorted(range(peers), key=lambda index: listed(index, peers))
    for k, index in enumerate(order):
        first = half if index & PAIR else 0
        packed_ref[k, :half] = back[first : first + half]
        packed_ref[k, half:] = weight[listed(index % owners, owners, corner=True)].astype(BF16)
    dpre_ref[...] = dpre


def input_kernel(targets_ref, back_ref, pair_ref, tiles_ref, dpre_ref, w_self_ref, total_ref, dest_ref, padded_ref, sem):
    copy = pltpu.make_async_copy(targets_ref, dest_ref, sem)
    copy.start()
    half = tiles_ref.shape[2] // 2
    _, sibling = halves(tiles_ref.shape[2])
    quarter = half // 2
    first = lax.axis_index("feat") * half
    odd = (lax.axis_index("dom") // PAIR) & 1
    padded_ref[:, pl.ds(pl.multiple_of(first + odd * quarter, quarter), quarter), :] = back_ref[...]
    padded_ref[:, pl.ds(pl.multiple_of(first + (1 - odd) * quarter, quarter), quarter), :] = pair_ref[...]
    padded_ref[:, sibling, :] = jnp.zeros((padded_ref.shape[0], half, padded_ref.shape[2]), BF16)
    peers = padded_ref.shape[0]
    total = dot(dpre_ref[...], w_self_ref[...], NT)
    copy.wait()
    if tiles_ref.shape[0] <= 16:
        for t in range(tiles_ref.shape[0]):
            total = total + dot(tiles_ref[t], padded_ref[listed(dest_ref[t], peers)], NN)
    else:
        total = lax.fori_loop(
            0, tiles_ref.shape[0], lambda t, sum: sum + dot(tiles_ref[t], padded_ref[listed(dest_ref[t], peers)], NN), total
        )
    total_ref[...] = total


def spread_kernel(back_ref, parts_ref):
    _, slab, _ = parts_ref.shape
    half = back_ref.shape[2] // 4
    part = jnp.sum(back_ref[:, half : half + slab].astype(F32), axis=0).astype(BF16)
    parts_ref[...] = jnp.broadcast_to(part[None], parts_ref.shape)


def output_kernel(silu_ref, term_ref, other_ref, weight_ref, output_ref, grad_input_ref, grad_self_ref, grad_neigh_ref):
    output_ref[...] = silu_ref[...]
    fin = grad_self_ref.shape[0]
    grad_input_ref[...] = (term_ref[...] + other_ref[...]).astype(BF16)
    grad_self_ref[...] = weight_ref[:fin].astype(F32)
    grad_neigh_ref[...] = weight_ref[fin:].astype(F32)


def on_device(features, w_self, w_neigh, tiles, dest, outside, cotangent):
    peers = lax.axis_size("dom")
    tile_count, rows, _ = tiles.shape
    fin, hidden = w_self.shape
    half = fin // 2
    slab = 2 * fin // (peers // SHARERS)
    vmem = pl.BlockSpec(memory_space=pltpu.VMEM)
    hbm = pl.BlockSpec(memory_space=pltpu.HBM)
    targets = dest.reshape(-1)
    shape = jax.ShapeDtypeStruct

    def swap(x):
        return lax.ppermute(x, "feat", [(0, 1), (1, 0)])

    def exchange(x, groups):
        return lax.all_to_all(x, "dom", split_axis=0, concat_axis=0, tiled=True, axis_index_groups=groups)

    middle = [sorted(range(peers), key=lambda index: listed(index, peers))]
    owners = peers // SHARERS
    corner = sorted(range(owners), key=lambda index: listed(index, owners, corner=True))
    corner = [[first + index for index in corner] for first in range(0, peers, owners)]
    extended = half + EXTRA
    share, outside, targets = pl.pallas_call(
        share_kernel,
        out_shape=(
            pltpu.VMEM((peers, extended, rows), BF16),
            pltpu.VMEM((1, rows), jnp.int32),
            pltpu.VMEM((tile_count,), jnp.int32),
        ),
        in_specs=[hbm] * 4,
        out_specs=(vmem,) * 3,
        scratch_shapes=[
            pltpu.SMEM((tile_count,), jnp.int32),
            pltpu.VMEM((rows, fin), BF16),
            pltpu.VMEM(tiles.shape, BF16),
            pltpu.VMEM((fin, rows), BF16),
            pltpu.VMEM((peers, extended, rows), F32),
            pltpu.SemaphoreType.DMA((5,)),
        ],
        compiler_params=pltpu.CompilerParams(vmem_limit_bytes=60 * MIB),
        name="share",
    )(targets, features, outside.reshape(1, rows), tiles)
    arrived = exchange(share, middle)
    together = half + 2 * fin + rows // 2
    total, links = pl.pallas_call(
        sum_kernel,
        out_shape=(pltpu.VMEM((together, hidden), BF16), pltpu.VMEM((EXTRA, rows), F32)),
        in_specs=[vmem] * 4,
        out_specs=(vmem,) * 2,
        compiler_params=pltpu.CompilerParams(vmem_limit_bytes=(4 + peers // 8) * MIB),
        name="sum",
    )(arrived, w_self, w_neigh, cotangent)
    output, packed, dpre = pl.pallas_call(
        node_kernel,
        out_shape=(
            pltpu.VMEM((rows, hidden), BF16),
            pltpu.VMEM((peers, rows // 4 + max(slab, 16), hidden), BF16),
            pltpu.VMEM((rows, hidden), BF16),
        ),
        in_specs=[vmem] * 8,
        out_specs=(vmem,) * 3,
        scratch_shapes=[
            pltpu.VMEM((fin, rows), BF16),
            pltpu.VMEM((rows, fin), BF16),
            pltpu.VMEM((rows, hidden), F32),
            pltpu.VMEM((rows, hidden), BF16),
        ],
        compiler_params=pltpu.CompilerParams(vmem_limit_bytes=(4 + peers // 8) * MIB),
        name="node",
    )(total, swap(total), links, outside, features, w_self, w_neigh, cotangent)
    back = exchange(packed, middle)
    half_back = back[:, : rows // 4]
    summed = pl.pallas_call(
        spread_kernel,
        out_shape=pltpu.VMEM((owners, slab, hidden), BF16),
        in_specs=[vmem],
        out_specs=vmem,
        compiler_params=pltpu.CompilerParams(vmem_limit_bytes=(4 + peers // 16) * MIB),
        name="spread",
    )(back)
    summed, half_back = lax.optimization_barrier((summed, half_back))
    pair = lax.ppermute(half_back, "dom", [(i, i ^ PAIR) for i in range(peers)])
    weight = exchange(summed, corner)
    term = pl.pallas_call(
        input_kernel,
        out_shape=shape((rows, fin), F32),
        in_specs=[vmem] * 6,
        out_specs=vmem,
        scratch_shapes=[
            pltpu.SMEM((tile_count,), jnp.int32),
            pltpu.VMEM((peers, rows, fin), BF16),
            pltpu.SemaphoreType.DMA,
        ],
        compiler_params=pltpu.CompilerParams(vmem_limit_bytes=(4 + peers // 8) * MIB),
        name="input",
    )(targets, half_back, pair, tiles, dpre, w_self)
    block = shape((fin, hidden), F32)
    return pl.pallas_call(
        output_kernel,
        out_shape=(shape((rows, hidden), BF16), shape((rows, fin), BF16), block, block),
        in_specs=[vmem] * 4,
        out_specs=(vmem,) * 4,
        compiler_params=pltpu.CompilerParams(vmem_limit_bytes=4 * MIB),
        name="outputs",
    )(output, term, swap(term), weight.reshape(2 * fin, hidden))


def solution(mesh):
    placed = (
        P("dom", None),
        P(None, "feat"),
        P(None, "feat"),
        P("dom", None, None),
        P("dom", None),
        P("dom"),
        P("dom", "feat"),
    )
    return jax.shard_map(
        on_device,
        mesh=mesh,
        in_specs=placed,
        out_specs=(P("dom", "feat"), P("dom", None), P(None, "feat"), P(None, "feat")),
        check_vma=False,
    )
```

```python
import jax
import jax.numpy as jnp
from jax import lax
from jax.experimental import pallas as pl
from jax.experimental.pallas import tpu as pltpu
from jax.sharding import PartitionSpec as P

BF16 = jnp.bfloat16
F32 = jnp.float32
EXTRA = 8
SHARERS = 2
PAIR = 4
MIB = 1 << 20

NN = (((1,), (0,)), ((), ()))
NT = (((1,), (1,)), ((), ()))


def dot(a, b, dims):
    return lax.dot_general(a, b, dims, preferred_element_type=F32)


def loop(count, body):
    if count <= 16:
        for index in range(count):
            body(index)
    else:
        pl.loop(0, count)(body)


def listed(index, peers, corner=False, near=False):
    bits = peers.bit_length() - 1
    index = index ^ (peers - 1 if corner else peers // 2 - 1 if near else peers - peers // 4 - 1)
    return sum(((index >> bit) & 1) << (bits - 1 - bit) for bit in range(bits))


def halves(size):
    core = lax.axis_index("feat")
    half = size // 2
    return pl.ds(pl.multiple_of(core * half, half), half), pl.ds(pl.multiple_of((1 - core) * half, half), half)


def share_kernel(
    dest_hbm, features_hbm, outside_hbm, tiles_hbm, share_ref, outside_ref, targets_ref, dest_ref, features_ref, tiles_ref, turned_ref, sums_ref, sems,
):
    copies = [
        pltpu.make_async_copy(source, target, sems.at[i])
        for i, (source, target) in enumerate(
            [
                (tiles_hbm, tiles_ref), (features_hbm, features_ref), (dest_hbm, dest_ref),
                (outside_hbm, outside_ref), (dest_hbm, targets_ref),
            ]
        )
    ]
    for copy in copies:
        copy.start()
    peers = sums_ref.shape[0]
    sums_ref[...] = jnp.zeros_like(sums_ref)
    copies[1].wait()
    turned_ref[...] = features_ref[...].T
    own, _ = halves(turned_ref.shape[0])
    left = jnp.concatenate([turned_ref[own, :], jnp.ones((EXTRA, turned_ref.shape[1]), BF16)], axis=0)
    copies[2].wait()
    copies[0].wait()

    def add(t):
        sums_ref[listed(dest_ref[t], peers)] += dot(left, tiles_ref[t], NN)

    loop(tiles_ref.shape[0], add)
    share_ref[...] = sums_ref[...].astype(BF16)
    copies[3].wait()
    copies[4].wait()


def sum_kernel(arrived_ref, w_self_ref, w_neigh_ref, cotangent_ref, total_ref, links_ref):
    half = arrived_ref.shape[1] - EXTRA
    fin = w_self_ref.shape[0]
    total = jnp.sum(arrived_ref[...].astype(F32), axis=0)
    links_ref[...] = total[half:]
    total_ref[:half] = total[:half].astype(BF16)
    total_ref[half : half + fin] = w_self_ref[...]
    total_ref[half + fin : half + 2 * fin] = w_neigh_ref[...]
    _, sibling = halves(cotangent_ref.shape[0])
    total_ref[half + 2 * fin :] = cotangent_ref[sibling, :]


def node_kernel(
    total_ref, other_ref, links_ref, outside_ref, features_ref, w_self_ref, w_neigh_ref, cotangent_ref,
    output_ref, packed_ref, dpre_ref, gathered_ref, nodes_ref, scale_ref, dagg_ref,
):
    fin, rows = gathered_ref.shape
    hidden = w_self_ref.shape[1]
    quarter = fin // 2
    own, sibling = halves(fin)
    low, _ = halves(rows)
    gathered_ref[own, :] = total_ref[:quarter]
    gathered_ref[sibling, :] = other_ref[:quarter]
    gathered = gathered_ref[...]
    nodes_ref[...] = gathered.T
    degree = links_ref[0:1] + outside_ref[...].astype(F32)
    scale_ref[...] = jnp.broadcast_to(1.0 / degree, (hidden, rows)).T

    def gradients(features, nodes, scale, w_self, w_neigh, cotangent):
        pre = dot(features, w_self, NN) + dot(nodes, w_neigh, NN) * scale
        sigma = 1.0 / (1.0 + jnp.exp(-pre))
        dpre = (cotangent.astype(F32) * sigma * (1.0 + pre * (1.0 - sigma))).astype(BF16)
        return pre * sigma, dpre, (dpre.astype(F32) * scale).astype(BF16)

    features, w_neigh = features_ref[...], w_neigh_ref[...]
    silu, dpre, dagg = gradients(
        features, nodes_ref[...], scale_ref[...], w_self_ref[...], w_neigh, cotangent_ref[...]
    )
    output_ref[...] = silu.astype(BF16)
    dagg_ref[...] = dagg
    w_self_other = other_ref[quarter : quarter + fin]
    w_neigh_other = other_ref[quarter + fin : quarter + 2 * fin]
    _, _, dagg_other = gradients(
        features_ref[low, :], nodes_ref[low, :], scale_ref[low, :], w_self_other, w_neigh_other,
        other_ref[quarter + 2 * fin :],
    )
    back = dot(dagg_ref[low, :], w_neigh, NT) + dot(dagg_other, w_neigh_other, NT)
    peers, packed, _ = packed_ref.shape
    owners = peers // SHARERS
    slab = 2 * fin // owners
    half = rows // 4
    back = back.astype(BF16)
    weight = jnp.concatenate([dot(features.T, dpre, NN), dot(gathered, dagg, NN)], axis=0)
    weight = weight.reshape(owners, slab, hidden)
    if packed - half > slab:
        weight = jnp.concatenate([weight, jnp.zeros((owners, packed - half - slab, hidden), F32)], axis=1)
    order = sorted(range(peers), key=lambda index: listed(index, peers, near=True))
    for k, index in enumerate(order):
        first = half if index & PAIR else 0
        packed_ref[k, :half] = back[first : first + half]
        packed_ref[k, half:] = weight[listed(index % owners, owners, corner=True)].astype(BF16)
    dpre_ref[...] = dpre


def input_kernel(targets_ref, back_ref, pair_ref, tiles_ref, dpre_ref, w_self_ref, total_ref, dest_ref, padded_ref, sem):
    copy = pltpu.make_async_copy(targets_ref, dest_ref, sem)
    copy.start()
    half = tiles_ref.shape[2] // 2
    _, sibling = halves(tiles_ref.shape[2])
    quarter = half // 2
    first = lax.axis_index("feat") * half
    odd = (lax.axis_index("dom") // PAIR) & 1
    padded_ref[:, pl.ds(pl.multiple_of(first + odd * quarter, quarter), quarter), :] = back_ref[...]
    padded_ref[:, pl.ds(pl.multiple_of(first + (1 - odd) * quarter, quarter), quarter), :] = pair_ref[...]
    padded_ref[:, sibling, :] = jnp.zeros((padded_ref.shape[0], half, padded_ref.shape[2]), BF16)
    peers = padded_ref.shape[0]
    total = dot(dpre_ref[...], w_self_ref[...], NT)
    copy.wait()
    if tiles_ref.shape[0] <= 16:
        for t in range(tiles_ref.shape[0]):
            total = total + dot(tiles_ref[t], padded_ref[listed(dest_ref[t], peers, near=True)], NN)
    else:
        total = lax.fori_loop(
            0, tiles_ref.shape[0], lambda t, sum: sum + dot(tiles_ref[t], padded_ref[listed(dest_ref[t], peers, near=True)], NN), total
        )
    total_ref[...] = total


def spread_kernel(back_ref, parts_ref):
    _, slab, _ = parts_ref.shape
    half = back_ref.shape[2] // 4
    part = jnp.sum(back_ref[:, half : half + slab].astype(F32), axis=0).astype(BF16)
    parts_ref[...] = jnp.broadcast_to(part[None], parts_ref.shape)


def output_kernel(silu_ref, term_ref, other_ref, weight_ref, output_ref, grad_input_ref, grad_self_ref, grad_neigh_ref):
    output_ref[...] = silu_ref[...]
    fin = grad_self_ref.shape[0]
    grad_input_ref[...] = (term_ref[...] + other_ref[...]).astype(BF16)
    grad_self_ref[...] = weight_ref[:fin].astype(F32)
    grad_neigh_ref[...] = weight_ref[fin:].astype(F32)


def on_device(features, w_self, w_neigh, tiles, dest, outside, cotangent):
    peers = lax.axis_size("dom")
    tile_count, rows, _ = tiles.shape
    fin, hidden = w_self.shape
    half = fin // 2
    slab = 2 * fin // (peers // SHARERS)
    vmem = pl.BlockSpec(memory_space=pltpu.VMEM)
    hbm = pl.BlockSpec(memory_space=pltpu.HBM)
    targets = dest.reshape(-1)
    shape = jax.ShapeDtypeStruct

    def swap(x):
        return lax.ppermute(x, "feat", [(0, 1), (1, 0)])

    def exchange(x, groups):
        return lax.all_to_all(x, "dom", split_axis=0, concat_axis=0, tiled=True, axis_index_groups=groups)

    middle = [sorted(range(peers), key=lambda index: listed(index, peers))]
    near = [sorted(range(peers), key=lambda index: listed(index, peers, near=True))]
    owners = peers // SHARERS
    corner = sorted(range(owners), key=lambda index: listed(index, owners, corner=True))
    corner = [[first + index for index in corner] for first in range(0, peers, owners)]
    extended = half + EXTRA
    share, outside, targets = pl.pallas_call(
        share_kernel,
        out_shape=(
            pltpu.VMEM((peers, extended, rows), BF16),
            pltpu.VMEM((1, rows), jnp.int32),
            pltpu.VMEM((tile_count,), jnp.int32),
        ),
        in_specs=[hbm] * 4,
        out_specs=(vmem,) * 3,
        scratch_shapes=[
            pltpu.SMEM((tile_count,), jnp.int32),
            pltpu.VMEM((rows, fin), BF16),
            pltpu.VMEM(tiles.shape, BF16),
            pltpu.VMEM((fin, rows), BF16),
            pltpu.VMEM((peers, extended, rows), F32),
            pltpu.SemaphoreType.DMA((5,)),
        ],
        compiler_params=pltpu.CompilerParams(vmem_limit_bytes=60 * MIB),
        name="share",
    )(targets, features, outside.reshape(1, rows), tiles)
    arrived = exchange(share, middle)
    together = half + 2 * fin + rows // 2
    total, links = pl.pallas_call(
        sum_kernel,
        out_shape=(pltpu.VMEM((together, hidden), BF16), pltpu.VMEM((EXTRA, rows), F32)),
        in_specs=[vmem] * 4,
        out_specs=(vmem,) * 2,
        compiler_params=pltpu.CompilerParams(vmem_limit_bytes=(4 + peers // 8) * MIB),
        name="sum",
    )(arrived, w_self, w_neigh, cotangent)
    output, packed, dpre = pl.pallas_call(
        node_kernel,
        out_shape=(
            pltpu.VMEM((rows, hidden), BF16),
            pltpu.VMEM((peers, rows // 4 + max(slab, 16), hidden), BF16),
            pltpu.VMEM((rows, hidden), BF16),
        ),
        in_specs=[vmem] * 8,
        out_specs=(vmem,) * 3,
        scratch_shapes=[
            pltpu.VMEM((fin, rows), BF16),
            pltpu.VMEM((rows, fin), BF16),
            pltpu.VMEM((rows, hidden), F32),
            pltpu.VMEM((rows, hidden), BF16),
        ],
        compiler_params=pltpu.CompilerParams(vmem_limit_bytes=(4 + peers // 8) * MIB),
        name="node",
    )(total, swap(total), links, outside, features, w_self, w_neigh, cotangent)
    back = exchange(packed, near)
    half_back = back[:, : rows // 4]
    pair = lax.ppermute(half_back, "dom", [(i, i ^ PAIR) for i in range(peers)])
    summed = pl.pallas_call(
        spread_kernel,
        out_shape=pltpu.VMEM((owners, slab, hidden), BF16),
        in_specs=[vmem],
        out_specs=vmem,
        compiler_params=pltpu.CompilerParams(vmem_limit_bytes=(4 + peers // 16) * MIB),
        name="spread",
    )(back)
    summed, half_back = lax.optimization_barrier((summed, half_back))
    weight = exchange(summed, corner)
    term = pl.pallas_call(
        input_kernel,
        out_shape=shape((rows, fin), F32),
        in_specs=[vmem] * 6,
        out_specs=vmem,
        scratch_shapes=[
            pltpu.SMEM((tile_count,), jnp.int32),
            pltpu.VMEM((peers, rows, fin), BF16),
            pltpu.SemaphoreType.DMA,
        ],
        compiler_params=pltpu.CompilerParams(vmem_limit_bytes=(4 + peers // 8) * MIB),
        name="input",
    )(targets, half_back, pair, tiles, dpre, w_self)
    block = shape((fin, hidden), F32)
    return pl.pallas_call(
        output_kernel,
        out_shape=(shape((rows, hidden), BF16), shape((rows, fin), BF16), block, block),
        in_specs=[vmem] * 4,
        out_specs=(vmem,) * 4,
        compiler_params=pltpu.CompilerParams(vmem_limit_bytes=4 * MIB),
        name="outputs",
    )(output, term, swap(term), weight.reshape(2 * fin, hidden))


def solution(mesh):
    placed = (
        P("dom", None),
        P(None, "feat"),
        P(None, "feat"),
        P("dom", None, None),
        P("dom", None),
        P("dom"),
        P("dom", "feat"),
    )
    return jax.shard_map(
        on_device,
        mesh=mesh,
        in_specs=placed,
        out_specs=(P("dom", "feat"), P("dom", None), P(None, "feat"), P(None, "feat")),
        check_vma=False,
    )
```
